128 devices in a mesh: row: 16 (over x, z), col: 8 (over y, core).
Axes of the slice: x: 4, y: 4, z: 4, core: 2. Of those that a mesh axis runs over, the one named last changes fastest.
Arguments:
- front: bfloat16 [16384, 16384], P('row', 'col'), may hold values from -6 to 6
- tiles: bfloat16 [16384, 128, 128], P(('row', 'col')), may hold values from -6 to 6
- counts: int32 [128], P(('row', 'col')), may hold values from 64 to 128, as said below
- dest_owner: int32 [16384, 1], P(('row', 'col')), may hold values from 0 to 127; in each aligned block of 128 rows (0 to 127, 128 to 255, ...) at most 2 rows name the same one
- dest_slot: int32 [16384], P(('row', 'col')), may hold values from 0 to 127
- omega: bfloat16 [512, 128], replicated, may hold values from -0.25 to 0.25
- psi: bfloat16 [512, 128], replicated, may hold values from -0.25 to 0.25
- core: bfloat16 [128, 128], replicated, may hold values from -0.00390625 to 0.00390625
Outputs:
- updated: bfloat16 [16384, 16384], P('row', 'col')
The draws below stay inside these ranges and needn't reach their ends.
Inputs may be any that keep to these rules, and one draw needn't show every extreme that they name: `counts`: some device has all 128 tiles live in every draw. `dest_owner`: among the 128 tiles of one device at most 2 name the same owner, live or not; this is reached.
All inputs are finite; a program needn't handle non-finite values.
Results may differ from the reference program's by a relative error of at most 0.0085.
Values may be sent and summed in bfloat16 or wider, within the bound.
A program may use at most 128 MiB of HBM per device.

```python
import math
import jax
import jax.numpy as jnp
import numpy as np

N = 16384
PB = 512
SK = 128
TILE = 128
PANELS = 10
CAP = 2
STRIPS = 128
TILES_DEV = 128
N_ROW = 16
N_COL = 8
DEVICES = 128


def draw_counts(key, part):
    key = jax.random.fold_in(key, 7)
    first, second = jax.random.split(key)
    values = jax.random.randint(first, (DEVICES,), STRIPS // 2, STRIPS + 1)
    chosen = jax.random.randint(second, (), 0, DEVICES)
    return values.at[chosen].set(STRIPS).astype(jnp.int32)


def touch_ends(drawn, rng, least, top_value):
    place = [jax.random.randint(jax.random.fold_in(rng, axis), (), 0, length) for axis, length in enumerate(drawn.shape)]
    main_axis = drawn.shape.index(max(drawn.shape))
    neighbour = place[:main_axis] + [(place[main_axis] + 1) % drawn.shape[main_axis]] + place[main_axis + 1:]
    return drawn.at[tuple(place)].set(least).at[tuple(neighbour)].set(top_value)


def level_of(rng, extent, shards, least, largest):
    level = 1.0
    for dim, shards_of in shards:
        steps = jax.random.uniform(jax.random.fold_in(jax.random.fold_in(rng, 6), dim), (shards_of,), jnp.float32, least / len(shards), largest / len(shards))
        level = level * jnp.repeat(jnp.exp(steps), extent[dim] // shards_of).reshape((-1,) + (1,) * (len(extent) - 1 - dim))
    return level


def deal_out(stream_key, own, number, rows, count, top, limit, slope):
    ranking = jax.random.permutation(stream_key, count)
    heavy_load, common = portions_of(count, rows * top, limit, slope, True), portions_of(count, rows * top, limit, slope, False)
    places = jnp.arange(count)

    def named(lengths, rotation):
        used = int((lengths > 0).sum())
        fixed = max(1, used // 4)
        passed = fixed + (places - fixed + rotation * (used - fixed)) % max(1, count - fixed)
        return jnp.zeros((count,), jnp.int32).at[ranking[jnp.where(places < fixed, places, passed)]].set(jnp.asarray(lengths, jnp.int32))

    lengths = jnp.where(number % 4 == 0, named(heavy_load, number // 4), named(common, number - number // 4 - 1))
    mixed = jax.random.permutation(jax.random.fold_in(own, 3), count)
    giver, receiver = mixed[0:count // 2 * 2:2], mixed[1:count // 2 * 2:2]
    slack = jnp.minimum(lengths[giver] - 1, limit - lengths[receiver]) // 2
    slack = jnp.where((giver == ranking[0]) | (receiver == ranking[0]) | (lengths[receiver] == 0), 0, jnp.maximum(slack, 0))
    passed = jax.random.randint(jax.random.fold_in(own, 4), (count // 2,), 0, 1 << 20) % (slack + 1)
    lengths = lengths.at[giver].add(-passed).at[receiver].add(passed)
    items = jnp.searchsorted(jnp.cumsum(lengths), jnp.arange(rows * top), side="right").astype(jnp.int32)
    listing = items.reshape(top, rows).T
    listing = listing[jax.random.permutation(jax.random.fold_in(own, 1), rows)]
    rotation = jax.random.randint(jax.random.fold_in(own, 2), (rows, 1), 0, top)
    return jnp.take_along_axis(listing, (jnp.arange(top)[None, :] + rotation) % top, axis=1)


def portions_of(amount, total, bound, skew, full):
    weights = [(1 << 20) // math.isqrt(standing ** skew) + 1 for standing in range(1, amount + 1)]
    largest = bound if full else min(bound, max(-(-total // amount), total * weights[0] // sum(weights)))
    least = 1 if total - largest >= amount - 1 else 0
    given, surplus = [largest] + [least] * (amount - 1), total - largest - least * (amount - 1)
    while surplus > 0:
        movable = [i for i in range(1, amount) if given[i] < largest] or [i for i in range(1, amount) if given[i] < bound]
        mass, remaining = sum([weights[i] for i in movable]), surplus
        for i in movable:
            more = min(bound - given[i], max(1, remaining * weights[i] // mass), surplus)
            given[i] = given[i] + more
            surplus = surplus - more
    return np.array(given)


def normal_values(own_key, extent, spread, bound, cuts=(), held_as=jnp.bfloat16):
    level = level_of(own_key, extent, cuts, -0.22, 0.18) if cuts else 1.0
    array = jax.random.normal(own_key, extent, jnp.float32) * spread * level
    return jnp.minimum(jnp.maximum(array, -bound), bound).astype(held_as)


def setup_inputs(seed: int = 0) -> dict:
    streams_of = jax.random.split(jax.random.key(seed), 9)
    front = normal_values(streams_of[0], (N, N), 1.0, 6.0, ((0, 16), (1, 8)))
    tiles = normal_values(streams_of[1], (DEVICES * STRIPS, TILE, TILE), 1.0, 6.0, ((0, 128),))
    counts = draw_counts(jax.random.fold_in(streams_of[8], 71), 0)
    dest_owner_keys = jax.random.split(jax.random.fold_in(streams_of[3], 1), (DEVICES * STRIPS) // STRIPS)
    dest_owner_turns = jax.random.permutation(jax.random.fold_in(streams_of[3], 3), (DEVICES * STRIPS) // STRIPS)
    dest_owner = jax.vmap(lambda own, number: deal_out(jax.random.fold_in(streams_of[3], 2), own, number, STRIPS, DEVICES, 1, CAP, 2))(dest_owner_keys, dest_owner_turns).reshape((DEVICES * STRIPS, 1))
    dest_slot = touch_ends(jax.random.randint(streams_of[4], (DEVICES * STRIPS,), 0, TILES_DEV), jax.random.fold_in(streams_of[4], 1), 0, TILES_DEV - 1).astype(jnp.int32)
    omega = normal_values(streams_of[5], (PB, SK), PB ** -0.5, 0.25)
    psi = normal_values(streams_of[6], (PB, SK), PB ** -0.5, 0.25)
    core = normal_values(streams_of[7], (SK, SK), (SK * N) ** -0.5, 0.00390625)
    return {"front": front, "tiles": tiles, "counts": counts, "dest_owner": dest_owner, "dest_slot": dest_slot, "omega": omega, "psi": psi, "core": core}


def reference(front, tiles, counts, dest_owner, dest_slot, omega, psi, core):
    n_tiles = N // TILE
    col_tiles = N // N_COL // TILE
    row_tiles = N // N_ROW // TILE
    total = N_ROW * N_COL * STRIPS
    index = jnp.arange(total, dtype=jnp.int32)
    valid = (index % STRIPS) < counts[index // STRIPS]
    owner = dest_owner[:, 0]
    tile_row = (owner // N_COL) * row_tiles + dest_slot // col_tiles
    tile_col = (owner % N_COL) * col_tiles + dest_slot % col_tiles
    values = jnp.where(valid[:, None, None], tiles.astype(jnp.float32), jnp.float32(0.0))
    grid = front.astype(jnp.float32).reshape(n_tiles, TILE, n_tiles, TILE)
    grid = grid.at[tile_row, :, tile_col, :].add(values).reshape(N, N)
    position = jnp.arange(N, dtype=jnp.int32)
    for panel in range(PANELS):
        lower = panel * PB
        upper = lower + PB
        pcols = grid[:, lower:upper].astype(jnp.bfloat16)
        basis = jnp.dot(pcols, omega, preferred_element_type=jnp.float32).astype(jnp.bfloat16)
        left = jnp.dot(basis, core, preferred_element_type=jnp.float32).astype(jnp.bfloat16)
        prows = grid[lower:upper, :].astype(jnp.bfloat16)
        right = jnp.dot(psi.T, prows, preferred_element_type=jnp.float32).astype(jnp.bfloat16)
        keep = (position >= upper).astype(jnp.float32)
        grid = grid - jnp.dot(left, right, preferred_element_type=jnp.float32) * keep[:, None] * keep[None, :]
    return grid.astype(jnp.bfloat16)
```

```python
import functools

import jax
import jax.numpy as jnp
from jax import lax
from jax.experimental import pallas as pl
from jax.experimental.pallas import tpu as pltpu
from jax.sharding import PartitionSpec as P

PB = 512
SK = 128
TILE = 128
PANELS = 10
CAP = 2
ND = 128
NR = 16
NC = 8
ROWS = 1024
COLS = 2048
RANK = PANELS * SK
RSRC = 5
CSRC = 3
MESH = pl.DeviceIdType.MESH
MIB = 2**20


def div(a, b):
    return lax.div(a, jnp.int32(b))


def rem(a, b):
    return lax.rem(a, jnp.int32(b))


def partner(me, step):
    j = rem(step * 31, 128)
    bit = lambda p: rem(div(j, 2**p), 2)
    dx = bit(5) * 2 + bit(2)
    dz = bit(0) * 2 + bit(1)
    dy = bit(6) * 2 + bit(4)
    dk = bit(3)
    x = rem(div(me, 32) + dx, 4)
    z = rem(div(me, 8) + dz, 4)
    y = rem(div(me, 2) + dy, 4)
    k = rem(me + dk, 2)
    return x * 32 + z * 8 + y * 2 + k


def exchange_kernel(
    idx_ref, slot_ref, tiles_ref, got_ref, gslot_ref, send, held, lsem, ssem, rsem, slot_ssem, slot_rsem
):
    me = lax.axis_index("row") * NC + lax.axis_index("col")
    load = pltpu.make_async_copy(tiles_ref, held, lsem.at[0])
    load.start()
    barrier = pltpu.get_barrier_semaphore()

    def greet(step, carry):
        p = partner(me, step)
        pl.semaphore_signal(barrier, inc=1, device_id=(div(p, NC), rem(p, NC)), device_id_type=MESH)
        return carry

    lax.fori_loop(1, ND, greet, 0)
    own_slot = pltpu.make_async_copy(slot_ref.at[me], gslot_ref.at[me], lsem.at[1])
    own_slot.start()
    load.wait()

    def pack(p):
        for k in range(CAP):
            send[p, k] = held[idx_ref[k, p]]

    pack(me)
    own = pltpu.make_async_copy(send.at[me], got_ref.at[me], lsem.at[2])
    own.start()
    pl.semaphore_wait(barrier, ND - 1)

    def copies(p, landing):
        device = (div(p, NC), rem(p, NC))
        tile = pltpu.make_async_remote_copy(
            src_ref=send.at[p], dst_ref=got_ref.at[landing], send_sem=ssem.at[p], recv_sem=rsem.at[landing],
            device_id=device, device_id_type=MESH,
        )
        slot = pltpu.make_async_remote_copy(
            src_ref=slot_ref.at[p], dst_ref=gslot_ref.at[landing], send_sem=slot_ssem.at[p],
            recv_sem=slot_rsem.at[landing], device_id=device, device_id_type=MESH,
        )
        return tile, slot

    def post(step, carry):
        p = partner(me, step)
        pack(p)
        tile, slot = copies(p, me)
        tile.start()
        slot.start()
        return carry

    lax.fori_loop(1, ND, post, 0)

    def finish(step, carry):
        p = partner(me, step)
        tile, slot = copies(p, p)
        tile.wait()
        slot.wait()
        return carry

    lax.fori_loop(1, ND, finish, 0)
    own_slot.wait()
    own.wait()


def exchange(idx, slots, tiles):
    any_spec = pl.BlockSpec(memory_space=pl.ANY)
    return pl.pallas_call(
        exchange_kernel,
        out_shape=(
            jax.ShapeDtypeStruct((ND, CAP, TILE, TILE), jnp.bfloat16),
            jax.ShapeDtypeStruct((ND, 1, TILE), jnp.int32),
        ),
        in_specs=[pl.BlockSpec(memory_space=pltpu.SMEM), any_spec, any_spec],
        out_specs=(any_spec, any_spec),
        scratch_shapes=[
            pltpu.VMEM((ND, CAP, TILE, TILE), jnp.bfloat16),
            pltpu.VMEM((ND, TILE, TILE), jnp.bfloat16),
            pltpu.SemaphoreType.DMA((3,)),
            pltpu.SemaphoreType.DMA((ND,)),
            pltpu.SemaphoreType.DMA((ND,)),
            pltpu.SemaphoreType.DMA((ND,)),
            pltpu.SemaphoreType.DMA((ND,)),
        ],
        compiler_params=pltpu.CompilerParams(
            collective_id=0, has_side_effects=True, vmem_limit_bytes=32 * MIB
        ),
        name="tile_exchange",
    )(idx, slots, tiles)


CHUNK = 8


def assemble_kernel(
    slot_ref, front_ref, got_ref, omega_ref, psi_ref, grid_ref, b_ref, s_ref, t_ref, grid, front, got, fsem, gsem, osem
):
    r = lax.axis_index("row")
    c = lax.axis_index("col")
    n_chunks = ND // CHUNK
    load_front = pltpu.make_async_copy(front_ref, front, fsem)
    load_front.start()
    loads = [
        pltpu.make_async_copy(got_ref.at[pl.ds(i * CHUNK, CHUNK)], got.at[pl.ds(i * CHUNK, CHUNK)], gsem.at[i])
        for i in range(n_chunks)
    ]
    for load in loads:
        load.start()
    load_front.wait()

    def widen(i, carry):
        rows = pl.ds(pl.multiple_of(i * 64, 64), 64)
        grid[rows, :] = front[rows, :].astype(jnp.float32)
        return carry

    lax.fori_loop(0, ROWS // 64, widen, 0)

    def add(source, carry):
        @pl.when(rem(source, CHUNK) == 0)
        def _():
            chunk = div(source, CHUNK)
            pltpu.make_async_copy(
                got_ref.at[pl.ds(source, CHUNK)], got.at[pl.ds(source, CHUNK)], gsem.at[chunk]
            ).wait()

        for k in range(CAP):
            slot = slot_ref[source, k]

            @pl.when(slot >= 0)
            def _():
                rows = pl.ds(pl.multiple_of(div(slot, COLS // TILE) * TILE, TILE), TILE)
                cols = pl.ds(pl.multiple_of(rem(slot, COLS // TILE) * TILE, TILE), TILE)
                grid[rows, cols] += got[source, k].astype(jnp.float32)

        return carry

    lax.fori_loop(0, ND, add, 0)
    store = pltpu.make_async_copy(grid, grid_ref, osem)
    store.start()

    @pl.when(c < CSRC)
    def _():
        def rows_of(i, carry):
            rows = pl.ds(pl.multiple_of(i * 256, 256), 256)
            for k in range(4):
                block = grid[rows, k * PB : (k + 1) * PB].astype(jnp.bfloat16)
                b_ref[rows, k * SK : (k + 1) * SK] = jnp.dot(
                    block, omega_ref[...], preferred_element_type=jnp.float32
                ).astype(jnp.bfloat16)
            return carry

        lax.fori_loop(0, ROWS // 256, rows_of, 0)

    @pl.when(r < RSRC)
    def _():
        psi_t = psi_ref[...].T
        for j in range(2):
            def cols_of(i, carry):
                cols = pl.ds(pl.multiple_of(i * 512, 512), 512)
                block = grid[j * PB : (j + 1) * PB, cols].astype(jnp.bfloat16)
                s_ref[j * SK : (j + 1) * SK, cols] = jnp.dot(
                    psi_t, block, preferred_element_type=jnp.float32
                ).astype(jnp.bfloat16)
                return carry

            lax.fori_loop(0, COLS // 512, cols_of, 0)

        @pl.when(c < CSRC)
        def _():
            for j in range(2):
                t_ref[j * SK : (j + 1) * SK, :] = jnp.dot(
                    psi_t, b_ref[j * PB : (j + 1) * PB, :], preferred_element_type=jnp.float32
                ).astype(jnp.bfloat16)

    store.wait()


def assemble(slots, front, got, omega, psi):
    any_spec = pl.BlockSpec(memory_space=pl.ANY)
    vmem = pl.BlockSpec(memory_space=pltpu.VMEM)
    return pl.pallas_call(
        assemble_kernel,
        out_shape=(
            jax.ShapeDtypeStruct((ROWS, COLS), jnp.float32),
            jax.ShapeDtypeStruct((ROWS, 4 * SK), jnp.bfloat16),
            jax.ShapeDtypeStruct((2 * SK, COLS), jnp.bfloat16),
            jax.ShapeDtypeStruct((2 * SK, 4 * SK), jnp.bfloat16),
        ),
        in_specs=[pl.BlockSpec(memory_space=pltpu.SMEM), any_spec, any_spec, vmem, vmem],
        out_specs=(any_spec, vmem, vmem, vmem),
        scratch_shapes=[
            pltpu.VMEM((ROWS, COLS), jnp.float32),
            pltpu.VMEM((ROWS, COLS), jnp.bfloat16),
            pltpu.VMEM((ND, CAP, TILE, TILE), jnp.bfloat16),
            pltpu.SemaphoreType.DMA,
            pltpu.SemaphoreType.DMA((ND // CHUNK,)),
            pltpu.SemaphoreType.DMA,
        ],
        compiler_params=pltpu.CompilerParams(vmem_limit_bytes=40 * MIB),
        name="extend_add",
    )(slots, front, got, omega, psi)


TR = 2 * SK // NC


def gather_kernel(
    b_ref, s_ref, t_ref, ball, sall, tall,
    lsem, t1s, t1r, t2s, t2r, t3s, t3r, bss, bsr, bas, bar, sss, ssr, sas, sar,
):
    r = lax.axis_index("row")
    c = lax.axis_index("col")
    x, z = div(r, 4), rem(r, 4)
    y, k = div(c, 2), rem(c, 2)

    barrier = pltpu.get_barrier_semaphore()
    for i in range(1, NR):
        pl.semaphore_signal(barrier, inc=1, device_id=(rem(r + i, NR), c), device_id_type=MESH)
    for i in range(1, NC):
        pl.semaphore_signal(barrier, inc=1, device_id=(r, rem(c + i, NC)), device_id_type=MESH)
    pl.semaphore_wait(barrier, NR - 1 + NC - 1)

    def remote(src, dst, send, recv, device):
        return pltpu.make_async_remote_copy(
            src_ref=src, dst_ref=dst, send_sem=send, recv_sem=recv, device_id=device, device_id_type=MESH
        )

    def t1(cc, src_c, width, sem):
        return remote(
            t_ref.at[pl.ds(pl.multiple_of(cc * TR, TR), TR), pl.ds(0, width)],
            tall.at[cc, r, :, pl.ds(src_c * 4 * SK, width)],
            t1s.at[sem], t1r.at[src_c], (r, cc),
        )

    def b1(cc, src_c, width, sem):
        return remote(
            b_ref.at[pl.ds(pl.multiple_of(cc * TILE, TILE), TILE), pl.ds(0, width)],
            ball.at[cc, :, pl.ds(src_c * 4 * SK, width)],
            bss.at[sem], bsr.at[src_c], (r, cc),
        )

    def s1(rr, sem):
        return remote(
            s_ref.at[:, pl.ds(pl.multiple_of(rr * TILE, TILE), TILE)], sall.at[rr, r],
            sss.at[sem], ssr.at[r], (rr, c),
        )

    widths = [4 * SK, 4 * SK, 2 * SK]

    def own_t(src_c):
        w = widths[src_c]
        return pltpu.make_async_copy(
            t_ref.at[pl.ds(pl.multiple_of(c * TR, TR), TR), pl.ds(0, w)],
            tall.at[c, r, :, pl.ds(src_c * 4 * SK, w)], lsem.at[0],
        )

    def own_b(src_c):
        w = widths[src_c]
        return pltpu.make_async_copy(
            b_ref.at[pl.ds(pl.multiple_of(c * TILE, TILE), TILE), pl.ds(0, w)],
            ball.at[c, :, pl.ds(src_c * 4 * SK, w)], lsem.at[1],
        )

    def own_s():
        return pltpu.make_async_copy(
            s_ref.at[:, pl.ds(pl.multiple_of(r * TILE, TILE), TILE)], sall.at[r, r], lsem.at[2]
        )

    @pl.when(r < RSRC)
    def _():
        for src_c in range(CSRC):
            @pl.when(c == src_c)
            def _():
                own_t(src_c).start()
                for i in range(1, NC):
                    t1(rem(c + i, NC), src_c, widths[src_c], i).start()

    for src_c in range(CSRC):
        @pl.when(c == src_c)
        def _():
            own_b(src_c).start()
            for i in range(1, NC):
                b1(rem(c + i, NC), src_c, widths[src_c], i).start()

    @pl.when(r < RSRC)
    def _():
        own_s().start()
        for i in range(1, NR):
            s1(rem(r + i, NR), i).start()

    def t2(src_r, rr, sem):
        return remote(tall.at[c, src_r], tall.at[c, src_r], t2s.at[sem], t2r.at[src_r], (rr, c))

    @pl.when(r < RSRC)
    def _():
        for src_c in range(CSRC):
            @pl.when(c != src_c)
            def _():
                t1(c, src_c, widths[src_c], 0).wait_recv()

            @pl.when(c == src_c)
            def _():
                own_t(src_c).wait()
        for i in range(1, NR):
            t2(r, rem(r + i, NR), i).start()

    def along(axis, d):
        if axis == "x":
            return rem(x + d, 4) * 4 + z
        return x * 4 + rem(z + d, 4)

    def s2(half, piece, rr, sem):
        part = sall.at[piece, :, pl.ds(half * SK, SK), :]
        return remote(part, part, sas.at[half, sem], sar.at[half, piece], (rr, c))

    for src_r in range(RSRC):
        @pl.when(r != src_r)
        def _():
            remote(
                s_ref.at[:, pl.ds(0, TILE)], sall.at[r, src_r], sss.at[0], ssr.at[src_r], (r, c)
            ).wait_recv()

        @pl.when(r == src_r)
        def _():
            own_s().wait()

    axes = (("x", "z"), ("z", "x"))
    order = (1, 3, 2)
    for n, d in enumerate(order):
        for half in range(2):
            s2(half, r, along(axes[half][0], d), n).start()

    def t3(piece, cc, sem):
        return remote(tall.at[piece], tall.at[piece], t3s.at[sem], t3r.at[piece], (r, cc))

    def b3(piece, cc, sem):
        return remote(ball.at[piece], ball.at[piece], bas.at[sem], bar.at[piece], (r, cc))

    for src_r in range(RSRC):
        @pl.when(r != src_r)
        def _():
            t2(src_r, r, 0).wait_recv()
    other = y * 2 + (1 - k)
    for n, d in enumerate(order):
        t3(c, rem(y + d, 4) * 2 + k, n).start()
    t3(c, other, 3).start()

    for n, d in enumerate(order):
        for half in range(2):
            s2(half, r, along(axes[half][1], d), 3 + n).start()

    for src_c in range(CSRC):
        @pl.when(c != src_c)
        def _():
            b1(c, src_c, widths[src_c], 0).wait_recv()

        @pl.when(c == src_c)
        def _():
            own_b(src_c).wait()
    for n, d in enumerate(order):
        b3(c, rem(y + d, 4) * 2 + k, n).start()
    b3(c, other, 3).start()

    for m, dd in enumerate(order):
        for half in range(2):
            piece = along(axes[half][0], dd)
            s2(half, piece, r, 0).wait_recv()
            for n, d in enumerate(order):
                s2(half, piece, along(axes[half][1], d), 6 + 3 * m + n).start()
    for m, dd in enumerate(order):
        piece = rem(y + dd, 4) * 2 + k
        t3(piece, c, 0).wait_recv()
        t3(piece, other, 4 + m).start()
    for m, dd in enumerate(order):
        piece = rem(y + dd, 4) * 2 + k
        b3(piece, c, 0).wait_recv()
        b3(piece, other, 4 + m).start()

    for yy in range(4):
        piece = yy * 2 + (1 - k)
        t3(piece, c, 0).wait_recv()
        b3(piece, c, 0).wait_recv()
    for dd in (1, 3, 2):
        for half in range(2):
            first, second = axes[half]
            for d in range(4):
                if first == "x":
                    piece = rem(x + d, 4) * 4 + rem(z + dd, 4)
                else:
                    piece = rem(x + dd, 4) * 4 + rem(z + d, 4)
                s2(half, piece, r, 0).wait_recv()

    @pl.when(r < RSRC)
    def _():
        for src_c in range(CSRC):
            @pl.when(c == src_c)
            def _():
                for i in range(1, NC):
                    t1(rem(c + i, NC), src_c, widths[src_c], i).wait_send()
        for i in range(1, NR):
            s1(rem(r + i, NR), i).wait_send()
            t2(r, rem(r + i, NR), i).wait_send()

    for src_c in range(CSRC):
        @pl.when(c == src_c)
        def _():
            for i in range(1, NC):
                b1(rem(c + i, NC), src_c, widths[src_c], i).wait_send()
    for i in range(7):
        t3(c, other, i).wait_send()
        b3(c, other, i).wait_send()
    for half in range(2):
        for i in range(15):
            s2(half, r, rem(r + 1, NR), i).wait_send()


def gather(b, s, t):
    any_spec = pl.BlockSpec(memory_space=pl.ANY)
    dma = pltpu.SemaphoreType.DMA
    return pl.pallas_call(
        gather_kernel,
        out_shape=(
            jax.ShapeDtypeStruct((NC, TILE, RANK), jnp.bfloat16),
            jax.ShapeDtypeStruct((NR, RSRC, 2 * SK, TILE), jnp.bfloat16),
            jax.ShapeDtypeStruct((NC, RSRC, TR, RANK), jnp.bfloat16),
        ),
        in_specs=[any_spec] * 3,
        out_specs=(any_spec,) * 3,
        scratch_shapes=[
            dma((3,)),
            dma((NC,)), dma((CSRC,)), dma((NR,)), dma((RSRC,)), dma((7,)), dma((NC,)),
            dma((NC,)), dma((CSRC,)), dma((7,)), dma((NC,)),
            dma((NR,)), dma((RSRC,)), dma((2, 15)), dma((2, NR)),
        ],
        compiler_params=pltpu.CompilerParams(collective_id=1, has_side_effects=True),
        name="sketch_gather",
    )(b, s, t)


UR = 256


def update_kernel(
    ball_ref, sall_ref, tall_ref, core_ref, grid_ref, out_ref,
    ball, sall, tall, state, left, right, wmat, vmat, gbuf, obuf, lsem, ssem, tsem, gsem, osem,
):
    r = lax.axis_index("row")
    c = lax.axis_index("col")
    f32 = jnp.float32
    bf16 = jnp.bfloat16
    t_loads = [
        pltpu.make_async_copy(tall_ref.at[cc], tall.at[:, pl.ds(cc * TR, TR), :], tsem.at[cc]) for cc in range(NC)
    ]
    for load in t_loads:
        load.start()
    b_load = pltpu.make_async_copy(ball_ref, ball, lsem)
    b_load.start()
    s_loads = [
        pltpu.make_async_copy(sall_ref.at[p], sall.at[:, :, pl.ds(p * TILE, TILE)], ssem.at[p]) for p in range(NR)
    ]
    for load in s_loads:
        load.start()
    g_loads = [
        pltpu.make_async_copy(grid_ref.at[pl.ds(i * UR, UR)], gbuf.at[i], gsem.at[i]) for i in range(ROWS // UR)
    ]
    for load in g_loads:
        load.start()
    for load in t_loads:
        load.wait()
    core = core_ref[...]

    for q in range(RSRC):
        state[q * 256 : (q + 1) * 256, :] = tall[q].astype(f32)
    for s in range(PANELS - 1):
        lo, hi = s * SK, (s + 1) * SK
        wmat[lo:hi, hi:] = state[lo:hi, hi:].astype(bf16)
        vmat[hi:, lo:hi] = jnp.dot(state[hi:, lo:hi].astype(bf16), core, preferred_element_type=f32).astype(bf16)
        if s < PANELS - 2:
            state[hi:, hi:] -= jnp.dot(vmat[hi:, lo:hi], wmat[lo:hi, hi:], preferred_element_type=f32)

    b_load.wait()
    for s in range(PANELS):
        lo, hi = s * SK, (s + 1) * SK

        def left_rows(i, carry):
            rows = pl.ds(pl.multiple_of(i * 512, 512), 512)
            basis = ball[rows, lo:hi].astype(f32)
            if s:
                basis -= jnp.dot(left[rows, :lo], wmat[:lo, lo:hi], preferred_element_type=f32)
            left[rows, lo:hi] = jnp.dot(basis.astype(bf16), core, preferred_element_type=f32).astype(bf16)
            return carry

        lax.fori_loop(0, ROWS // 512, left_rows, 0)

    for load in s_loads:
        load.wait()
    for s in range(PANELS):
        lo, hi = s * SK, (s + 1) * SK

        def right_cols(i, carry):
            cols = pl.ds(pl.multiple_of(i * 512, 512), 512)
            block = sall[s // 2, (s % 2) * SK : (s % 2 + 1) * SK, cols].astype(f32)
            if s:
                block -= jnp.dot(vmat[lo:hi, :lo], right[:lo, cols], preferred_element_type=f32)
            right[lo:hi, cols] = block.astype(bf16)
            return carry

        lax.fori_loop(0, COLS // 512, right_cols, 0)

    @pl.when(r < RSRC)
    def _():
        row_pos = r * ROWS + lax.broadcasted_iota(jnp.int32, (ROWS, SK), 0)
        for s in range(PANELS):
            block = left[:, s * SK : (s + 1) * SK]
            left[:, s * SK : (s + 1) * SK] = jnp.where(row_pos >= (s + 1) * PB, block, jnp.zeros_like(block))

    @pl.when(c < CSRC)
    def _():
        col_pos = c * COLS + lax.broadcasted_iota(jnp.int32, (SK, COLS), 1)
        for s in range(PANELS):
            block = right[s * SK : (s + 1) * SK, :]
            right[s * SK : (s + 1) * SK, :] = jnp.where(col_pos >= (s + 1) * PB, block, jnp.zeros_like(block))

    stores = []
    for i in range(ROWS // UR):
        g_loads[i].wait()
        rows = slice(i * UR, (i + 1) * UR)

        def cols_of(q, carry):
            cols = pl.ds(pl.multiple_of(q * 512, 512), 512)
            product = jnp.dot(left[rows, :], right[:, cols], preferred_element_type=f32)
            obuf[i, :, cols] = (gbuf[i, :, cols] - product).astype(bf16)
            return carry

        lax.fori_loop(0, COLS // 512, cols_of, 0)
        store = pltpu.make_async_copy(obuf.at[i], out_ref.at[pl.ds(i * UR, UR)], osem.at[i])
        store.start()
        stores.append(store)
    for store in stores:
        store.wait()


def update(ball, sall, tall, core, grid):
    any_spec = pl.BlockSpec(memory_space=pl.ANY)
    vmem = pl.BlockSpec(memory_space=pltpu.VMEM)
    dma = pltpu.SemaphoreType.DMA
    bf16 = jnp.bfloat16
    n = ROWS // UR
    return pl.pallas_call(
        update_kernel,
        out_shape=jax.ShapeDtypeStruct((ROWS, COLS), bf16),
        in_specs=[any_spec, any_spec, any_spec, vmem, any_spec],
        out_specs=any_spec,
        scratch_shapes=[
            pltpu.VMEM((ROWS, RANK), bf16),
            pltpu.VMEM((RSRC, 2 * SK, COLS), bf16),
            pltpu.VMEM((RSRC, 2 * SK, RANK), bf16),
            pltpu.VMEM((RANK, RANK), jnp.float32),
            pltpu.VMEM((ROWS, RANK), bf16),
            pltpu.VMEM((RANK, COLS), bf16),
            pltpu.VMEM((RANK, RANK), bf16),
            pltpu.VMEM((RANK, RANK), bf16),
            pltpu.VMEM((n, UR, COLS), jnp.float32),
            pltpu.VMEM((n, UR, COLS), bf16),
            dma, dma((NR,)), dma((NC,)), dma((n,)), dma((n,)),
        ],
        compiler_params=pltpu.CompilerParams(vmem_limit_bytes=56 * MIB),
        name="panel_update",
    )(ball, sall, tall, core, grid)


def shards(front, tiles, counts, dest_owner, dest_slot, omega, psi, core):
    owners = dest_owner[:, 0]
    strip = jnp.arange(ND, dtype=jnp.int32)
    same = owners[:, None] == owners[None, :]
    before = strip[None, :] < strip[:, None]
    ranks = jnp.sum((same & before).astype(jnp.int32), axis=1)
    valid = strip < counts[0]
    named = strip[None, :, None] == owners[None, None, :]
    hit = named & (ranks[None, None, :] == jnp.arange(CAP, dtype=jnp.int32)[:, None, None])
    idx = jnp.sum(jnp.where(hit, strip[None, None, :], 0), axis=2)
    slots = jnp.sum(jnp.where(hit & valid[None, None, :], dest_slot[None, None, :] + 1, 0), axis=2) - 1
    slots = jnp.pad(slots.T[:, None, :], ((0, 0), (0, 0), (0, TILE - CAP)))
    got, got_slots = exchange(idx, slots, tiles)
    grid, b, s, t = assemble(got_slots[:, 0, :], front, got, omega, psi)
    ball, sall, tall = gather(b, s, t)
    return update(ball.reshape(ROWS, RANK), sall, tall, core, grid)


def solution(mesh):
    in_specs = (
        P("row", "col"),
        P(("row", "col"), None, None),
        P(("row", "col")),
        P(("row", "col"), None),
        P(("row", "col")),
        P(),
        P(),
        P(),
    )
    out_specs = P("row", "col")
    return jax.shard_map(shards, mesh=mesh, in_specs=in_specs, out_specs=out_specs, check_vma=False)
```

```python
import functools

import jax
import jax.numpy as jnp
from jax import lax
from jax.experimental import pallas as pl
from jax.experimental.pallas import tpu as pltpu
from jax.sharding import PartitionSpec as P

PB = 512
SK = 128
TILE = 128
PANELS = 10
CAP = 2
ND = 128
NR = 16
NC = 8
ROWS = 1024
COLS = 2048
RANK = PANELS * SK
RSRC = 5
CSRC = 3
MESH = pl.DeviceIdType.MESH
MIB = 2**20


def div(a, b):
    return lax.div(a, jnp.int32(b))


def rem(a, b):
    return lax.rem(a, jnp.int32(b))


def partner(me, step):
    j = rem(step * 31, 128)
    bit = lambda p: rem(div(j, 2**p), 2)
    dx = bit(5) * 2 + bit(2)
    dz = bit(0) * 2 + bit(1)
    dy = bit(6) * 2 + bit(4)
    dk = bit(3)
    x = rem(div(me, 32) + dx, 4)
    z = rem(div(me, 8) + dz, 4)
    y = rem(div(me, 2) + dy, 4)
    k = rem(me + dk, 2)
    return x * 32 + z * 8 + y * 2 + k


def exchange_kernel(
    idx_ref, slot_ref, tiles_ref, got_ref, gslot_ref, send, lsem, ssem, rsem, slot_ssem, slot_rsem
):
    me = lax.axis_index("row") * NC + lax.axis_index("col")
    barrier = pltpu.get_barrier_semaphore()

    def greet(step, carry):
        p = partner(me, step)
        pl.semaphore_signal(barrier, inc=1, device_id=(div(p, NC), rem(p, NC)), device_id_type=MESH)
        return carry

    lax.fori_loop(1, ND, greet, 0)
    own_slot = pltpu.make_async_copy(slot_ref.at[me], gslot_ref.at[me], lsem.at[0])
    own_slot.start()

    def pack(p):
        for k in range(CAP):
            send[p, k] = tiles_ref[idx_ref[k, p]]

    pack(me)
    own = pltpu.make_async_copy(send.at[me], got_ref.at[me], lsem.at[1])
    own.start()
    pl.semaphore_wait(barrier, ND - 1)

    def copies(p, landing):
        device = (div(p, NC), rem(p, NC))
        tile = pltpu.make_async_remote_copy(
            src_ref=send.at[p], dst_ref=got_ref.at[landing], send_sem=ssem.at[p], recv_sem=rsem.at[landing],
            device_id=device, device_id_type=MESH,
        )
        slot = pltpu.make_async_remote_copy(
            src_ref=slot_ref.at[p], dst_ref=gslot_ref.at[landing], send_sem=slot_ssem.at[p],
            recv_sem=slot_rsem.at[landing], device_id=device, device_id_type=MESH,
        )
        return tile, slot

    def post(step, carry):
        p = partner(me, step)
        pack(p)
        tile, slot = copies(p, me)
        tile.start()
        slot.start()
        return carry

    lax.fori_loop(1, ND, post, 0)

    def finish(step, carry):
        p = partner(me, step)
        tile, slot = copies(p, p)
        tile.wait()
        slot.wait()
        return carry

    lax.fori_loop(1, ND, finish, 0)
    own_slot.wait()
    own.wait()


def exchange(idx, slots, tiles):
    vmem = pl.BlockSpec(memory_space=pltpu.VMEM)
    return pl.pallas_call(
        exchange_kernel,
        out_shape=(
            jax.ShapeDtypeStruct((ND, CAP, TILE, TILE), jnp.bfloat16),
            jax.ShapeDtypeStruct((ND, 1, TILE), jnp.int32),
        ),
        in_specs=[pl.BlockSpec(memory_space=pltpu.SMEM), vmem, vmem],
        out_specs=(vmem, vmem),
        scratch_shapes=[
            pltpu.VMEM((ND, CAP, TILE, TILE), jnp.bfloat16),
            pltpu.SemaphoreType.DMA((2,)),
            pltpu.SemaphoreType.DMA((ND,)),
            pltpu.SemaphoreType.DMA((ND,)),
            pltpu.SemaphoreType.DMA((ND,)),
            pltpu.SemaphoreType.DMA((ND,)),
        ],
        compiler_params=pltpu.CompilerParams(
            collective_id=0, has_side_effects=True, vmem_limit_bytes=12 * MIB
        ),
        name="tile_exchange",
    )(idx, slots, tiles)


def assemble_kernel(slot_ref, front_ref, got_ref, omega_ref, psi_ref, grid, b_ref, s_ref, t_ref):
    r = lax.axis_index("row")
    c = lax.axis_index("col")

    def widen(i, carry):
        rows = pl.ds(pl.multiple_of(i * 64, 64), 64)
        grid[rows, :] = front_ref[rows, :].astype(jnp.float32)
        return carry

    lax.fori_loop(0, ROWS // 64, widen, 0)

    def add(source, carry):
        for k in range(CAP):
            slot = slot_ref[source, k]

            @pl.when(slot >= 0)
            def _():
                rows = pl.ds(pl.multiple_of(div(slot, COLS // TILE) * TILE, TILE), TILE)
                cols = pl.ds(pl.multiple_of(rem(slot, COLS // TILE) * TILE, TILE), TILE)
                grid[rows, cols] += got_ref[source, k].astype(jnp.float32)

        return carry

    lax.fori_loop(0, ND, add, 0)

    @pl.when(c < CSRC)
    def _():
        def rows_of(i, carry):
            rows = pl.ds(pl.multiple_of(i * 256, 256), 256)
            for k in range(4):
                block = grid[rows, k * PB : (k + 1) * PB].astype(jnp.bfloat16)
                b_ref[rows, k * SK : (k + 1) * SK] = jnp.dot(
                    block, omega_ref[...], preferred_element_type=jnp.float32
                ).astype(jnp.bfloat16)
            return carry

        lax.fori_loop(0, ROWS // 256, rows_of, 0)

    @pl.when(r < RSRC)
    def _():
        psi_t = psi_ref[...].T
        for j in range(2):
            def cols_of(i, carry):
                cols = pl.ds(pl.multiple_of(i * 512, 512), 512)
                block = grid[j * PB : (j + 1) * PB, cols].astype(jnp.bfloat16)
                s_ref[j * SK : (j + 1) * SK, cols] = jnp.dot(
                    psi_t, block, preferred_element_type=jnp.float32
                ).astype(jnp.bfloat16)
                return carry

            lax.fori_loop(0, COLS // 512, cols_of, 0)

        @pl.when(c < CSRC)
        def _():
            for j in range(2):
                t_ref[j * SK : (j + 1) * SK, :] = jnp.dot(
                    psi_t, b_ref[j * PB : (j + 1) * PB, :], preferred_element_type=jnp.float32
                ).astype(jnp.bfloat16)


def assemble(slots, front, got, omega, psi):
    vmem = pl.BlockSpec(memory_space=pltpu.VMEM)
    return pl.pallas_call(
        assemble_kernel,
        out_shape=(
            jax.ShapeDtypeStruct((ROWS, COLS), jnp.float32),
            jax.ShapeDtypeStruct((ROWS, 4 * SK), jnp.bfloat16),
            jax.ShapeDtypeStruct((2 * SK, COLS), jnp.bfloat16),
            jax.ShapeDtypeStruct((2 * SK, 4 * SK), jnp.bfloat16),
        ),
        in_specs=[pl.BlockSpec(memory_space=pltpu.SMEM), vmem, vmem, vmem, vmem],
        out_specs=(vmem, vmem, vmem, vmem),
        compiler_params=pltpu.CompilerParams(vmem_limit_bytes=4 * MIB),
        name="extend_add",
    )(slots, front, got, omega, psi)


TR = 2 * SK // NC
WIDE = 4 * TILE
BLOCKS = COLS // WIDE
STEPS = (1, 3, 2)


def eliminate(tall, core, state, lmat, rmat):
    f32 = jnp.float32
    bf16 = jnp.bfloat16
    for cc in range(NC):
        for q in range(RSRC):
            lo = q * 2 * SK + cc * TR
            state[lo : lo + TR, :] = tall[cc, q].astype(f32)
    row = lax.broadcasted_iota(jnp.int32, (SK, SK), 0)
    col = lax.broadcasted_iota(jnp.int32, (SK, SK), 1)
    eye = jnp.where(row == col, 1.0, 0.0).astype(bf16)
    for s in range(PANELS):
        lo, hi = s * SK, (s + 1) * SK
        if s % 2 == 0:
            lmat[hi : hi + SK, lo:hi] = jnp.zeros((SK, SK), bf16)
            rmat[lo:hi, hi : hi + SK] = jnp.zeros((SK, SK), bf16)
        lmat[lo:hi, lo:hi] = core
        rmat[lo:hi, lo:hi] = eye
        if s:
            lmat[:lo, lo:hi] = jnp.dot(state[:lo, lo:hi].astype(bf16), core, preferred_element_type=f32).astype(bf16)
            rmat[lo:hi, :lo] = state[lo:hi, :lo].astype(bf16)
        if s == PANELS - 1:
            break
        below = jnp.dot(state[hi:, lo:hi].astype(bf16), core, preferred_element_type=f32).astype(bf16)
        beside = state[lo:hi, hi:].astype(bf16)
        state[hi:, hi:] -= jnp.dot(below, beside, preferred_element_type=f32)
        state[lo:hi, hi:] = -jnp.dot(core, beside, preferred_element_type=f32)
        state[hi:, lo:hi] = -below.astype(f32)
        if s:
            state[:lo, hi:] -= jnp.dot(lmat[:lo, lo:hi], beside, preferred_element_type=f32)
            state[hi:, :lo] -= jnp.dot(below, rmat[lo:hi, :lo], preferred_element_type=f32)


def factor_kernel(
    b_ref, s_ref, t_ref, core_ref, left, right,
    ball, sall, tall, state, lmat, rmat,
    lsem, t1s, t1r, t2s, t2r, t3s, t3r, bss, bsr, bas, bar, sss, ssr, s2s, s2r, s3s, s3r,
):
    r = lax.axis_index("row")
    c = lax.axis_index("col")
    x, z = div(r, 4), rem(r, 4)
    y, k = div(c, 2), rem(c, 2)
    other = y * 2 + (1 - k)
    f32 = jnp.float32
    bf16 = jnp.bfloat16

    barrier = pltpu.get_barrier_semaphore()
    for i in range(1, NR):
        pl.semaphore_signal(barrier, inc=1, device_id=(rem(r + i, NR), c), device_id_type=MESH)
    for i in range(1, NC):
        pl.semaphore_signal(barrier, inc=1, device_id=(r, rem(c + i, NC)), device_id_type=MESH)
    pl.semaphore_wait(barrier, NR - 1 + NC - 1)

    def remote(src, dst, send, recv, device):
        return pltpu.make_async_remote_copy(
            src_ref=src, dst_ref=dst, send_sem=send, recv_sem=recv, device_id=device, device_id_type=MESH
        )

    widths = [4 * SK, 4 * SK, 2 * SK]

    def t1(cc, src_c, sem):
        w = widths[src_c]
        return remote(
            t_ref.at[pl.ds(pl.multiple_of(cc * TR, TR), TR), pl.ds(0, w)],
            tall.at[cc, r, :, pl.ds(src_c * 4 * SK, w)],
            t1s.at[sem], t1r.at[src_c], (r, cc),
        )

    def b1(cc, src_c, sem):
        w = widths[src_c]
        return remote(
            b_ref.at[pl.ds(pl.multiple_of(cc * TILE, TILE), TILE), pl.ds(0, w)],
            ball.at[cc, :, pl.ds(src_c * 4 * SK, w)],
            bss.at[sem], bsr.at[src_c], (r, cc),
        )

    def s1(half, rr, src_r, sem):
        rows = pl.ds(half * SK, SK)
        return remote(
            s_ref.at[rows, pl.ds(pl.multiple_of(rr * TILE, TILE), TILE)], sall.at[rr, src_r, rows, :],
            sss.at[half, sem], ssr.at[half, src_r], (rr, c),
        )

    def own_t(src_c):
        w = widths[src_c]
        return pltpu.make_async_copy(
            t_ref.at[pl.ds(pl.multiple_of(c * TR, TR), TR), pl.ds(0, w)],
            tall.at[c, r, :, pl.ds(src_c * 4 * SK, w)], lsem.at[0],
        )

    def own_b(src_c):
        w = widths[src_c]
        return pltpu.make_async_copy(
            b_ref.at[pl.ds(pl.multiple_of(c * TILE, TILE), TILE), pl.ds(0, w)],
            ball.at[c, :, pl.ds(src_c * 4 * SK, w)], lsem.at[1],
        )

    def own_s():
        return pltpu.make_async_copy(
            s_ref.at[:, pl.ds(pl.multiple_of(r * TILE, TILE), TILE)], sall.at[r, r], lsem.at[2]
        )

    @pl.when(r < RSRC)
    def _():
        for src_c in range(CSRC):
            @pl.when(c == src_c)
            def _():
                own_t(src_c).start()
                for i in range(1, NC):
                    t1(rem(c + i, NC), src_c, i).start()

    for src_c in range(CSRC):
        @pl.when(c == src_c)
        def _():
            own_b(src_c).start()
            for i in range(1, NC):
                b1(rem(c + i, NC), src_c, i).start()

    homes = [(0, 0), (0, 1), (0, 2), (0, 3), (1, 0)]

    def t2(src_r, rr, sem):
        return remote(tall.at[c, src_r], tall.at[c, src_r], t2s.at[src_r, sem], t2r.at[src_r], (rr, c))

    @pl.when(r < RSRC)
    def _():
        for src_c in range(CSRC):
            @pl.when(c != src_c)
            def _():
                t1(c, src_c, 0).wait_recv()

            @pl.when(c == src_c)
            def _():
                own_t(src_c).wait()

    for src_r, (hx, hz) in enumerate(homes):
        @pl.when(r == src_r)
        def _():
            for n, d in enumerate(STEPS):
                t2(src_r, rem(x + d, 4) * 4 + z, n).start()
            for n, d in enumerate(STEPS):
                t2(src_r, x * 4 + rem(z + d, 4), 3 + n).start()

    axes = (("x", "z"), ("z", "x"))

    @pl.when(r < RSRC)
    def _():
        own_s().start()
        for half in range(2):
            for i in range(1, NR):
                s1(half, rem(r + i, NR), r, i).start()

    for src_r, (hx, hz) in enumerate(homes):
        @pl.when((z == hz) & (x != hx))
        def _():
            t2(src_r, r, 0).wait_recv()
            for n, d in enumerate(STEPS):
                t2(src_r, x * 4 + rem(z + d, 4), 3 + n).start()

    up = rem(y + 1, 4) * 2 + k
    down = rem(y + 3, 4) * 2 + k
    far = rem(y + 2, 4) * 2 + k

    def t3(piece, h, cc, sem):
        part = tall.at[piece, :, pl.ds(h * (TR // 2), TR // 2), :]
        return remote(part, part, t3s.at[sem], t3r.at[piece, h], (r, cc))

    def b3(piece, h, cc, sem):
        part = ball.at[piece, pl.ds(h * (TILE // 2), TILE // 2), :]
        return remote(part, part, bas.at[sem], bar.at[piece, h], (r, cc))

    def post_own(copy):
        copy(c, 0, up, 0).start()
        copy(c, 1, down, 1).start()
        copy(c, 1, up, 2).start()
        copy(c, 0, down, 3).start()
        copy(c, 0, other, 4).start()
        copy(c, 1, other, 5).start()

    def post_relays(copy):
        copy(down, 0, c, 0).wait_recv()
        copy(down, 0, up, 6).start()
        copy(down, 0, other, 7).start()
        copy(up, 1, c, 0).wait_recv()
        copy(up, 1, down, 8).start()
        copy(up, 1, other, 9).start()
        copy(down, 1, c, 0).wait_recv()
        copy(down, 1, other, 10).start()
        copy(up, 0, c, 0).wait_recv()
        copy(up, 0, other, 11).start()

    def post_far(copy):
        for h in range(2):
            copy(far, h, c, 0).wait_recv()
            copy(far, h, other, 12 + h).start()

    def wait_other(copy):
        for yy in range(4):
            for h in range(2):
                copy(yy * 2 + (1 - k), h, c, 0).wait_recv()

    for src_c in range(CSRC):
        @pl.when(c != src_c)
        def _():
            b1(c, src_c, 0).wait_recv()

        @pl.when(c == src_c)
        def _():
            own_b(src_c).wait()
    post_own(b3)

    for src_r, (hx, hz) in enumerate(homes):
        @pl.when(z != hz)
        def _():
            t2(src_r, r, 0).wait_recv()
    post_own(t3)

    def along(axis, d):
        if axis == "x":
            return rem(x + d, 4) * 4 + z
        return x * 4 + rem(z + d, 4)

    def first(half, piece, rr, sem):
        part = sall.at[piece, :, pl.ds(half * SK, SK), :]
        return remote(part, part, s2s.at[half, sem], s2r.at[half, piece], (rr, c))

    def second(half, piece, q, rr, sem):
        part = sall.at[piece, :, pl.ds(half * SK + q * (SK // 2), SK // 2), :]
        return remote(part, part, s3s.at[half, sem], s3r.at[half, piece, q], (rr, c))

    def post_second(half, piece, m):
        plus = along(axes[half][1], 1)
        minus = along(axes[half][1], 3)
        second(half, piece, 0, plus, 6 * m).start()
        second(half, piece, 1, minus, 6 * m + 1).start()
        second(half, piece, 1, plus, 6 * m + 2).start()
        second(half, piece, 0, minus, 6 * m + 3).start()

    def relay_second(half, d, m):
        for q, side, onward in ((0, 3, 1), (1, 1, 3)):
            if axes[half][0] == "x":
                piece = rem(x + d, 4) * 4 + rem(z + side, 4)
            else:
                piece = rem(x + side, 4) * 4 + rem(z + d, 4)
            second(half, piece, q, r, 0).wait_recv()
            second(half, piece, q, along(axes[half][1], onward), 6 * m + 4 + q).start()

    def settle(half, piece, distance):
        @pl.when(distance != 3)
        def _():
            second(half, piece, 0, r, 0).wait_recv()

        @pl.when(distance != 1)
        def _():
            second(half, piece, 1, r, 0).wait_recv()

    for half in range(2):
        for src_r in range(RSRC):
            @pl.when(r != src_r)
            def _():
                s1(half, r, src_r, 0).wait_recv()

            if half == 0:
                @pl.when(r == src_r)
                def _():
                    own_s().wait()
        for n, d in enumerate(STEPS):
            first(half, r, along(axes[half][0], d), n).start()
        post_second(half, r, 0)

    post_relays(b3)
    for half in range(2):
        relay_second(half, 0, 0)
    for m, d in enumerate(STEPS):
        for half in range(2):
            piece = along(axes[half][0], d)
            first(half, piece, r, 0).wait_recv()
            post_second(half, piece, 1 + m)
    post_relays(t3)
    post_far(b3)
    for half in range(2):
        relay_second(half, STEPS[0], 1)
    post_far(t3)
    for m in (1, 2):
        for half in range(2):
            relay_second(half, STEPS[m], 1 + m)
    wait_other(t3)

    core = core_ref[...]
    eliminate(tall, core, state, lmat, rmat)

    def right_block(i, carry):
        xx = rem(x + i, 4)
        for zz in range(4):
            piece = xx * 4 + zz
            dz = rem(zz - z + 4, 4)

            @pl.when(dz != 0)
            def _():
                settle(0, piece, dz)

            @pl.when(i != 0)
            def _():
                settle(1, piece, i)

        block = jnp.concatenate([sall[xx * 4 + h].reshape(RANK, TILE) for h in range(4)], axis=1)
        panel = c * (COLS // PB) + xx
        for q in range(RSRC):
            lo, hi = q * 2 * SK, (q + 1) * 2 * SK
            out = jnp.dot(rmat[lo:hi, :hi], block[:hi], preferred_element_type=f32)
            for j in range(2):
                part = out[j * SK : (j + 1) * SK]
                part = jnp.where(2 * q + j < panel, part, jnp.zeros_like(part))
                right[xx, lo + j * SK : lo + (j + 1) * SK, :] = part.astype(bf16)
        return carry

    lax.fori_loop(0, BLOCKS, right_block, 0)

    wait_other(b3)

    def left_rows(i, carry):
        panel = r * (ROWS // PB) + i
        block = jnp.concatenate([ball[i * 4 + h] for h in range(4)], axis=0)
        for q in range(RSRC):
            lo, hi = q * 2 * SK, (q + 1) * 2 * SK
            out = jnp.dot(block[:, :hi], lmat[:hi, lo:hi], preferred_element_type=f32)
            for j in range(2):
                part = out[:, j * SK : (j + 1) * SK]
                part = jnp.where(2 * q + j < panel, part, jnp.zeros_like(part))
                left[pl.ds(pl.multiple_of(i * PB, PB), PB), lo + j * SK : lo + (j + 1) * SK] = part.astype(bf16)
        return carry

    lax.fori_loop(0, ROWS // PB, left_rows, 0)

    @pl.when(r < RSRC)
    def _():
        for src_c in range(CSRC):
            @pl.when(c == src_c)
            def _():
                for i in range(1, NC):
                    t1(rem(c + i, NC), src_c, i).wait_send()
        for i in range(1, NR):
            for half in range(2):
                s1(half, rem(r + i, NR), r, i).wait_send()

    for src_c in range(CSRC):
        @pl.when(c == src_c)
        def _():
            for i in range(1, NC):
                b1(rem(c + i, NC), src_c, i).wait_send()
    for src_r, (hx, hz) in enumerate(homes):
        @pl.when(r == src_r)
        def _():
            for n in range(3):
                t2(src_r, rem(r + 1, NR), n).wait_send()

        @pl.when(z == hz)
        def _():
            for n in range(3):
                t2(src_r, rem(r + 1, NR), 3 + n).wait_send()
    for i in range(14):
        t3(c, 0, other, i).wait_send()
        b3(c, 0, other, i).wait_send()
    for half in range(2):
        for i in range(3):
            first(half, r, rem(r + 1, NR), i).wait_send()
        for i in range(24):
            second(half, r, 0, rem(r + 1, NR), i).wait_send()


def factors(b, s, t, core):
    vmem = pl.BlockSpec(memory_space=pltpu.VMEM)
    dma = pltpu.SemaphoreType.DMA
    bf16 = jnp.bfloat16
    return pl.pallas_call(
        factor_kernel,
        out_shape=(
            jax.ShapeDtypeStruct((ROWS, RANK), bf16),
            jax.ShapeDtypeStruct((BLOCKS, RANK, WIDE), bf16),
        ),
        in_specs=[vmem] * 4,
        out_specs=(vmem, vmem),
        scratch_shapes=[
            pltpu.VMEM((NC, TILE, RANK), bf16),
            pltpu.VMEM((NR, RSRC, 2 * SK, TILE), bf16),
            pltpu.VMEM((NC, RSRC, TR, RANK), bf16),
            pltpu.VMEM((RANK, RANK), jnp.float32),
            pltpu.VMEM((RANK, RANK), bf16),
            pltpu.VMEM((RANK, RANK), bf16),
            dma((3,)),
            dma((NC,)), dma((CSRC,)), dma((RSRC, 6)), dma((RSRC,)), dma((14,)), dma((NC, 2)),
            dma((NC,)), dma((CSRC,)), dma((14,)), dma((NC, 2)),
            dma((2, NR)), dma((2, RSRC)), dma((2, 3)), dma((2, NR)), dma((2, 24)), dma((2, NR, 2)),
        ],
        compiler_params=pltpu.CompilerParams(
            collective_id=1, has_side_effects=True, vmem_limit_bytes=28 * MIB
        ),
        name="panel_factors",
    )(b, s, t, core)


UR = 512


def update_kernel(left, right, grid, out_ref, obuf, osem):
    f32 = jnp.float32
    n = ROWS // UR

    def of_rows(i):
        return pl.ds(pl.multiple_of(i * UR, UR), UR)

    def store(i):
        return pltpu.make_async_copy(obuf.at[i], out_ref.at[of_rows(i)], osem.at[i])

    def rows(i, carry):
        def block(q, carry):
            cols = pl.ds(pl.multiple_of(q * WIDE, WIDE), WIDE)
            product = jnp.dot(left[of_rows(i), :], right[q], preferred_element_type=f32)
            obuf[i, :, cols] = (grid[of_rows(i), cols] - product).astype(jnp.bfloat16)
            return carry

        lax.fori_loop(0, BLOCKS, block, 0)
        store(i).start()
        return carry

    lax.fori_loop(0, n, rows, 0)
    for i in range(n):
        store(i).wait()


def update(left, right, grid):
    hbm = pl.BlockSpec(memory_space=pltpu.HBM)
    vmem = pl.BlockSpec(memory_space=pltpu.VMEM)
    n = ROWS // UR
    return pl.pallas_call(
        update_kernel,
        out_shape=jax.ShapeDtypeStruct((ROWS, COLS), jnp.bfloat16),
        in_specs=[vmem, vmem, vmem],
        out_specs=hbm,
        scratch_shapes=[pltpu.VMEM((n, UR, COLS), jnp.bfloat16), pltpu.SemaphoreType.DMA((n,))],
        compiler_params=pltpu.CompilerParams(vmem_limit_bytes=10 * MIB),
        name="panel_update",
    )(left, right, grid)


def shards(front, tiles, counts, dest_owner, dest_slot, omega, psi, core):
    owners = dest_owner[:, 0]
    strip = jnp.arange(ND, dtype=jnp.int32)
    same = owners[:, None] == owners[None, :]
    before = strip[None, :] < strip[:, None]
    ranks = jnp.sum((same & before).astype(jnp.int32), axis=1)
    valid = strip < counts[0]
    named = strip[None, :, None] == owners[None, None, :]
    hit = named & (ranks[None, None, :] == jnp.arange(CAP, dtype=jnp.int32)[:, None, None])
    idx = jnp.sum(jnp.where(hit, strip[None, None, :], 0), axis=2)
    slots = jnp.sum(jnp.where(hit & valid[None, None, :], dest_slot[None, None, :] + 1, 0), axis=2) - 1
    slots = jnp.pad(slots.T[:, None, :], ((0, 0), (0, 0), (0, TILE - CAP)))
    got, got_slots = exchange(idx, slots, tiles)
    grid, b, s, t = assemble(got_slots[:, 0, :], front, got, omega, psi)
    left, right = factors(b, s, t, core)
    return update(left, right, grid)


def solution(mesh):
    in_specs = (
        P("row", "col"),
        P(("row", "col"), None, None),
        P(("row", "col")),
        P(("row", "col"), None),
        P(("row", "col")),
        P(),
        P(),
        P(),
    )
    out_specs = P("row", "col")
    return jax.shard_map(shards, mesh=mesh, in_specs=in_specs, out_specs=out_specs, check_vma=False)
```

```python
import functools

import jax
import jax.numpy as jnp
from jax import lax
from jax.experimental import pallas as pl
from jax.experimental.pallas import tpu as pltpu
from jax.sharding import PartitionSpec as P

PB = 512
SK = 128
TILE = 128
PANELS = 10
CAP = 2
ND = 128
NR = 16
NC = 8
ROWS = 1024
COLS = 2048
RANK = PANELS * SK
RSRC = 5
CSRC = 3
MESH = pl.DeviceIdType.MESH
MIB = 2**20


def div(a, b):
    return lax.div(a, jnp.int32(b))


def rem(a, b):
    return lax.rem(a, jnp.int32(b))


def partner(me, step):
    j = rem(step * 31, 128)
    bit = lambda p: rem(div(j, 2**p), 2)
    dx = bit(0) * 2 + bit(3)
    dz = bit(5) * 2 + bit(4)
    dy = bit(6) * 2 + bit(2)
    dk = bit(1)
    x = rem(div(me, 32) + dx, 4)
    z = rem(div(me, 8) + dz, 4)
    y = rem(div(me, 2) + dy, 4)
    k = rem(me + dk, 2)
    return x * 32 + z * 8 + y * 2 + k


def exchange_kernel(
    idx_ref, slot_ref, tiles_ref, got_ref, gslot_ref, send, lsem, ssem, rsem, slot_ssem, slot_rsem
):
    me = lax.axis_index("row") * NC + lax.axis_index("col")
    barrier = pltpu.get_barrier_semaphore()

    def greet(step, carry):
        p = partner(me, step)
        pl.semaphore_signal(barrier, inc=1, device_id=(div(p, NC), rem(p, NC)), device_id_type=MESH)
        return carry

    lax.fori_loop(1, ND, greet, 0)
    own_slot = pltpu.make_async_copy(slot_ref.at[me], gslot_ref.at[me], lsem.at[0])
    own_slot.start()

    def pack(p):
        for k in range(CAP):
            send[p, k] = tiles_ref[idx_ref[k, p]]

    pack(me)
    own = pltpu.make_async_copy(send.at[me], got_ref.at[me], lsem.at[1])
    own.start()
    pl.semaphore_wait(barrier, ND - 1)

    def copies(p, landing):
        device = (div(p, NC), rem(p, NC))
        tile = pltpu.make_async_remote_copy(
            src_ref=send.at[p], dst_ref=got_ref.at[landing], send_sem=ssem.at[p], recv_sem=rsem.at[landing],
            device_id=device, device_id_type=MESH,
        )
        slot = pltpu.make_async_remote_copy(
            src_ref=slot_ref.at[p], dst_ref=gslot_ref.at[landing], send_sem=slot_ssem.at[p],
            recv_sem=slot_rsem.at[landing], device_id=device, device_id_type=MESH,
        )
        return tile, slot

    def post(step, carry):
        p = partner(me, step)
        pack(p)
        tile, slot = copies(p, me)
        tile.start()
        slot.start()
        return carry

    lax.fori_loop(1, ND, post, 0)

    def finish(step, carry):
        p = partner(me, step)
        tile, slot = copies(p, p)
        tile.wait()
        slot.wait()
        return carry

    lax.fori_loop(1, ND, finish, 0)
    own_slot.wait()
    own.wait()


def exchange(idx, slots, tiles):
    vmem = pl.BlockSpec(memory_space=pltpu.VMEM)
    return pl.pallas_call(
        exchange_kernel,
        out_shape=(
            jax.ShapeDtypeStruct((ND, CAP, TILE, TILE), jnp.bfloat16),
            jax.ShapeDtypeStruct((ND, 1, TILE), jnp.int32),
        ),
        in_specs=[pl.BlockSpec(memory_space=pltpu.SMEM), vmem, vmem],
        out_specs=(vmem, vmem),
        scratch_shapes=[
            pltpu.VMEM((ND, CAP, TILE, TILE), jnp.bfloat16),
            pltpu.SemaphoreType.DMA((2,)),
            pltpu.SemaphoreType.DMA((ND,)),
            pltpu.SemaphoreType.DMA((ND,)),
            pltpu.SemaphoreType.DMA((ND,)),
            pltpu.SemaphoreType.DMA((ND,)),
        ],
        compiler_params=pltpu.CompilerParams(
            collective_id=0, has_side_effects=True, vmem_limit_bytes=14 * MIB
        ),
        name="tile_exchange",
    )(idx, slots, tiles)


def assemble_kernel(slot_ref, front_ref, got_ref, omega_ref, psi_ref, grid, b_ref, s_ref, t_ref):
    r = lax.axis_index("row")
    c = lax.axis_index("col")

    def widen(i, carry):
        rows = pl.ds(pl.multiple_of(i * 64, 64), 64)
        grid[rows, :] = front_ref[rows, :].astype(jnp.float32)
        return carry

    lax.fori_loop(0, ROWS // 64, widen, 0)

    def add(source, carry):
        for k in range(CAP):
            slot = slot_ref[source, k]

            @pl.when(slot >= 0)
            def _():
                rows = pl.ds(pl.multiple_of(div(slot, COLS // TILE) * TILE, TILE), TILE)
                cols = pl.ds(pl.multiple_of(rem(slot, COLS // TILE) * TILE, TILE), TILE)
                grid[rows, cols] += got_ref[source, k].astype(jnp.float32)

        return carry

    lax.fori_loop(0, ND, add, 0)

    @pl.when(c < CSRC)
    def _():
        def rows_of(i, carry):
            rows = pl.ds(pl.multiple_of(i * 256, 256), 256)
            for k in range(4):
                block = grid[rows, k * PB : (k + 1) * PB].astype(jnp.bfloat16)
                b_ref[rows, k * SK : (k + 1) * SK] = jnp.dot(
                    block, omega_ref[...], preferred_element_type=jnp.float32
                ).astype(jnp.bfloat16)
            return carry

        lax.fori_loop(0, ROWS // 256, rows_of, 0)

    @pl.when(r < RSRC)
    def _():
        psi_t = psi_ref[...].T
        for j in range(2):
            def cols_of(i, carry):
                cols = pl.ds(pl.multiple_of(i * 512, 512), 512)
                block = grid[j * PB : (j + 1) * PB, cols].astype(jnp.bfloat16)
                s_ref[j * SK : (j + 1) * SK, cols] = jnp.dot(
                    psi_t, block, preferred_element_type=jnp.float32
                ).astype(jnp.bfloat16)
                return carry

            lax.fori_loop(0, COLS // 512, cols_of, 0)

        @pl.when(c < CSRC)
        def _():
            for j in range(2):
                t_ref[j * SK : (j + 1) * SK, :] = jnp.dot(
                    psi_t, b_ref[j * PB : (j + 1) * PB, :], preferred_element_type=jnp.float32
                ).astype(jnp.bfloat16)


def assemble(slots, front, got, omega, psi):
    vmem = pl.BlockSpec(memory_space=pltpu.VMEM)
    return pl.pallas_call(
        assemble_kernel,
        out_shape=(
            jax.ShapeDtypeStruct((ROWS, COLS), jnp.float32),
            jax.ShapeDtypeStruct((ROWS, 4 * SK), jnp.bfloat16),
            jax.ShapeDtypeStruct((2 * SK, COLS), jnp.bfloat16),
            jax.ShapeDtypeStruct((2 * SK, 4 * SK), jnp.bfloat16),
        ),
        in_specs=[pl.BlockSpec(memory_space=pltpu.SMEM), vmem, vmem, vmem, vmem],
        out_specs=(vmem, vmem, vmem, vmem),
        compiler_params=pltpu.CompilerParams(vmem_limit_bytes=6 * MIB),
        name="extend_add",
    )(slots, front, got, omega, psi)


TR = 2 * SK // NC
WIDE = 4 * TILE
BLOCKS = COLS // WIDE
STEPS = (1, 3, 2)
PLANE = (
    (1, 0), (3, 0), (0, 1), (2, 0), (1, 1), (3, 1), (0, 3), (2, 1),
    (1, 3), (3, 3), (0, 2), (2, 3), (1, 2), (3, 2), (2, 2),
)
LINE = ((1, 0), (3, 0), (1, 1), (3, 1), (2, 0), (2, 1), (0, 1))


def eliminate(tall, core, state, lmat, rmat, between):
    f32 = jnp.float32
    bf16 = jnp.bfloat16
    for cc in range(NC):
        for q in range(RSRC):
            lo = q * 2 * SK + cc * TR
            state[lo : lo + TR, :] = tall[cc, q].astype(f32)
    row = lax.broadcasted_iota(jnp.int32, (SK, SK), 0)
    col = lax.broadcasted_iota(jnp.int32, (SK, SK), 1)
    eye = jnp.where(row == col, 1.0, 0.0).astype(bf16)
    for s in range(PANELS):
        lo, hi = s * SK, (s + 1) * SK
        if s in between:
            between[s]()
        if s % 2 == 0:
            lmat[hi : hi + SK, lo:hi] = jnp.zeros((SK, SK), bf16)
            rmat[lo:hi, hi : hi + SK] = jnp.zeros((SK, SK), bf16)
        lmat[lo:hi, lo:hi] = core
        rmat[lo:hi, lo:hi] = eye
        if s:
            lmat[:lo, lo:hi] = jnp.dot(state[:lo, lo:hi].astype(bf16), core, preferred_element_type=f32).astype(bf16)
            rmat[lo:hi, :lo] = state[lo:hi, :lo].astype(bf16)
        if s == PANELS - 1:
            break
        below = jnp.dot(state[hi:, lo:hi].astype(bf16), core, preferred_element_type=f32).astype(bf16)
        beside = state[lo:hi, hi:].astype(bf16)
        state[hi:, hi:] -= jnp.dot(below, beside, preferred_element_type=f32)
        state[lo:hi, hi:] = -jnp.dot(core, beside, preferred_element_type=f32)
        state[hi:, lo:hi] = -below.astype(f32)
        if s:
            state[:lo, hi:] -= jnp.dot(lmat[:lo, lo:hi], beside, preferred_element_type=f32)
            state[hi:, :lo] -= jnp.dot(below, rmat[lo:hi, :lo], preferred_element_type=f32)


def factor_kernel(
    b_ref, s_ref, t_ref, core_ref, left, right,
    ball, sall, tall, state, lmat, rmat,
    lsem, t1s, t1r, t2s, t2r, t3s, t3r, bss, bsr, bas, bar, sss, ssr, s2s, s2r, s3s, s3r,
):
    r = lax.axis_index("row")
    c = lax.axis_index("col")
    x, z = div(r, 4), rem(r, 4)
    y, k = div(c, 2), rem(c, 2)
    other = y * 2 + (1 - k)
    f32 = jnp.float32
    bf16 = jnp.bfloat16

    barrier = pltpu.get_barrier_semaphore()
    for i in range(1, NR):
        pl.semaphore_signal(barrier, inc=1, device_id=(rem(r + i, NR), c), device_id_type=MESH)
    for i in range(1, NC):
        pl.semaphore_signal(barrier, inc=1, device_id=(r, rem(c + i, NC)), device_id_type=MESH)
    pl.semaphore_wait(barrier, NR - 1 + NC - 1)

    def remote(src, dst, send, recv, device):
        return pltpu.make_async_remote_copy(
            src_ref=src, dst_ref=dst, send_sem=send, recv_sem=recv, device_id=device, device_id_type=MESH
        )

    widths = [4 * SK, 4 * SK, 2 * SK]

    def t1(cc, src_c, sem):
        w = widths[src_c]
        return remote(
            t_ref.at[pl.ds(pl.multiple_of(cc * TR, TR), TR), pl.ds(0, w)],
            tall.at[cc, r, :, pl.ds(src_c * 4 * SK, w)],
            t1s.at[sem], t1r.at[src_c], (r, cc),
        )

    def b1(cc, src_c, sem):
        w = widths[src_c]
        return remote(
            b_ref.at[pl.ds(pl.multiple_of(cc * TILE, TILE), TILE), pl.ds(0, w)],
            ball.at[cc, :, pl.ds(src_c * 4 * SK, w)],
            bss.at[sem], bsr.at[src_c], (r, cc),
        )

    def s1(half, rr, src_r, sem):
        rows = pl.ds(half * SK, SK)
        return remote(
            s_ref.at[rows, pl.ds(pl.multiple_of(rr * TILE, TILE), TILE)], sall.at[rr, src_r, rows, :],
            sss.at[half, sem], ssr.at[half, src_r], (rr, c),
        )

    def own_t(src_c):
        w = widths[src_c]
        return pltpu.make_async_copy(
            t_ref.at[pl.ds(pl.multiple_of(c * TR, TR), TR), pl.ds(0, w)],
            tall.at[c, r, :, pl.ds(src_c * 4 * SK, w)], lsem.at[0],
        )

    def own_b(src_c):
        w = widths[src_c]
        return pltpu.make_async_copy(
            b_ref.at[pl.ds(pl.multiple_of(c * TILE, TILE), TILE), pl.ds(0, w)],
            ball.at[c, :, pl.ds(src_c * 4 * SK, w)], lsem.at[1],
        )

    def own_s():
        return pltpu.make_async_copy(
            s_ref.at[:, pl.ds(pl.multiple_of(r * TILE, TILE), TILE)], sall.at[r, r], lsem.at[2]
        )

    @pl.when(r < RSRC)
    def _():
        for src_c in range(CSRC):
            @pl.when(c == src_c)
            def _():
                own_t(src_c).start()
                for i, (dy, dk) in enumerate(LINE):
                    t1(rem(y + dy, 4) * 2 + rem(k + dk, 2), src_c, 1 + i).start()

    for src_c in range(CSRC):
        @pl.when(c == src_c)
        def _():
            own_b(src_c).start()
            for i, (dy, dk) in enumerate(LINE):
                b1(rem(y + dy, 4) * 2 + rem(k + dk, 2), src_c, 1 + i).start()

    homes = [(0, 0), (0, 1), (0, 2), (0, 3), (1, 0)]

    def t2(src_r, rr, sem):
        return remote(tall.at[c, src_r], tall.at[c, src_r], t2s.at[src_r, sem], t2r.at[src_r], (rr, c))

    @pl.when(r < RSRC)
    def _():
        for src_c in range(CSRC):
            @pl.when(c != src_c)
            def _():
                t1(c, src_c, 0).wait_recv()

            @pl.when(c == src_c)
            def _():
                own_t(src_c).wait()

    for src_r, (hx, hz) in enumerate(homes):
        @pl.when(r == src_r)
        def _():
            for n, d in enumerate(STEPS):
                t2(src_r, rem(x + d, 4) * 4 + z, n).start()
                t2(src_r, x * 4 + rem(z + d, 4), 3 + n).start()

    axes = (("x", "z"), ("z", "x"))

    @pl.when(r < RSRC)
    def _():
        own_s().start()
        for half in range(2):
            for i, (dx, dz) in enumerate(PLANE):
                s1(half, rem(x + dx, 4) * 4 + rem(z + dz, 4), r, 1 + i).start()

    for src_r, (hx, hz) in enumerate(homes):
        if src_r < 4:
            @pl.when((z == hz) & (x != hx))
            def _():
                t2(src_r, r, 0).wait_recv()
                for n, d in enumerate(STEPS):
                    t2(src_r, x * 4 + rem(z + d, 4), 3 + n).start()
        else:
            @pl.when((x == hx) & (z != hz))
            def _():
                t2(src_r, r, 0).wait_recv()
                for n, d in enumerate(STEPS):
                    t2(src_r, rem(x + d, 4) * 4 + z, n).start()

    up = rem(y + 1, 4) * 2 + k
    down = rem(y + 3, 4) * 2 + k
    far = rem(y + 2, 4) * 2 + k

    def t3(piece, h, cc, sem):
        part = tall.at[piece, :, pl.ds(h * (TR // 2), TR // 2), :]
        return remote(part, part, t3s.at[sem], t3r.at[piece, h], (r, cc))

    def b3(piece, h, cc, sem):
        part = ball.at[piece, pl.ds(h * (TILE // 2), TILE // 2), :]
        return remote(part, part, bas.at[sem], bar.at[piece, h], (r, cc))

    def post_own(copy):
        copy(c, 0, up, 0).start()
        copy(c, 1, down, 1).start()
        copy(c, 1, up, 2).start()
        copy(c, 0, down, 3).start()
        copy(c, 0, other, 4).start()
        copy(c, 1, other, 5).start()

    def post_relays(copy):
        copy(down, 0, c, 0).wait_recv()
        copy(down, 0, up, 6).start()
        copy(down, 0, other, 7).start()
        copy(up, 1, c, 0).wait_recv()
        copy(up, 1, down, 8).start()
        copy(up, 1, other, 9).start()
        copy(down, 1, c, 0).wait_recv()
        copy(down, 1, other, 10).start()
        copy(up, 0, c, 0).wait_recv()
        copy(up, 0, other, 11).start()

    def post_far(copy):
        for h in range(2):
            copy(far, h, c, 0).wait_recv()
            copy(far, h, other, 12 + h).start()

    def wait_other(copy):
        for yy in range(4):
            for h in range(2):
                copy(yy * 2 + (1 - k), h, c, 0).wait_recv()

    for src_c in range(CSRC):
        @pl.when(c != src_c)
        def _():
            b1(c, src_c, 0).wait_recv()

        @pl.when(c == src_c)
        def _():
            own_b(src_c).wait()
    post_own(b3)

    for src_r, (hx, hz) in enumerate(homes):
        @pl.when((z != hz) if src_r < 4 else (x != hx))
        def _():
            t2(src_r, r, 0).wait_recv()
    post_own(t3)

    def along(axis, d):
        if axis == "x":
            return rem(x + d, 4) * 4 + z
        return x * 4 + rem(z + d, 4)

    def first(half, piece, rr, sem):
        part = sall.at[piece, :, pl.ds(half * SK, SK), :]
        return remote(part, part, s2s.at[half, sem], s2r.at[half, piece], (rr, c))

    def second(half, piece, q, rr, sem):
        part = sall.at[piece, :, pl.ds(half * SK + q * (SK // 2), SK // 2), :]
        return remote(part, part, s3s.at[half, sem], s3r.at[half, piece, q], (rr, c))

    def post_second(half, piece, m):
        plus = along(axes[half][1], 1)
        minus = along(axes[half][1], 3)
        second(half, piece, 0, plus, 6 * m).start()
        second(half, piece, 1, minus, 6 * m + 1).start()
        second(half, piece, 1, plus, 6 * m + 2).start()
        second(half, piece, 0, minus, 6 * m + 3).start()

    def relay_second(half, d, m):
        for q, side, onward in ((0, 3, 1), (1, 1, 3)):
            if axes[half][0] == "x":
                piece = rem(x + d, 4) * 4 + rem(z + side, 4)
            else:
                piece = rem(x + side, 4) * 4 + rem(z + d, 4)
            second(half, piece, q, r, 0).wait_recv()
            second(half, piece, q, along(axes[half][1], onward), 6 * m + 4 + q).start()

    def settle(half, piece, distance):
        @pl.when(distance != 3)
        def _():
            second(half, piece, 0, r, 0).wait_recv()

        @pl.when(distance != 1)
        def _():
            second(half, piece, 1, r, 0).wait_recv()

    for half in range(2):
        for src_r in range(RSRC):
            @pl.when(r != src_r)
            def _():
                s1(half, r, src_r, 0).wait_recv()

            if half == 0:
                @pl.when(r == src_r)
                def _():
                    own_s().wait()
        for n, d in enumerate(STEPS):
            first(half, r, along(axes[half][0], d), n).start()
        post_second(half, r, 0)

    post_relays(b3)
    for half in range(2):
        relay_second(half, 0, 0)
    for m, d in enumerate(STEPS):
        for half in range(2):
            piece = along(axes[half][0], d)
            first(half, piece, r, 0).wait_recv()
            post_second(half, piece, 1 + m)
    post_relays(t3)
    post_far(b3)
    for half in range(2):
        relay_second(half, STEPS[0], 1)
    post_far(t3)
    wait_other(t3)

    def relay_both(m):
        for half in range(2):
            relay_second(half, STEPS[m], 1 + m)

    core = core_ref[...]
    eliminate(tall, core, state, lmat, rmat, {1: lambda: relay_both(1), 5: lambda: relay_both(2)})

    def right_block(i, carry):
        xx = rem(x + i, 4)
        for zz in range(4):
            piece = xx * 4 + zz
            dz = rem(zz - z + 4, 4)

            @pl.when(dz != 0)
            def _():
                settle(0, piece, dz)

            @pl.when(i != 0)
            def _():
                settle(1, piece, i)

        block = jnp.concatenate([sall[xx * 4 + h].reshape(RANK, TILE) for h in range(4)], axis=1)
        panel = c * (COLS // PB) + xx
        for q in range(RSRC):
            lo, hi = q * 2 * SK, (q + 1) * 2 * SK
            out = jnp.dot(rmat[lo:hi, :hi], block[:hi], preferred_element_type=f32)
            for j in range(2):
                part = out[j * SK : (j + 1) * SK]
                part = jnp.where(2 * q + j < panel, part, jnp.zeros_like(part))
                right[xx, lo + j * SK : lo + (j + 1) * SK, :] = part.astype(bf16)
        return carry

    lax.fori_loop(0, BLOCKS, right_block, 0)

    wait_other(b3)

    def left_rows(i, carry):
        panel = r * (ROWS // PB) + i
        block = jnp.concatenate([ball[i * 4 + h] for h in range(4)], axis=0)
        for q in range(RSRC):
            lo, hi = q * 2 * SK, (q + 1) * 2 * SK
            out = jnp.dot(block[:, :hi], lmat[:hi, lo:hi], preferred_element_type=f32)
            for j in range(2):
                part = out[:, j * SK : (j + 1) * SK]
                part = jnp.where(2 * q + j < panel, part, jnp.zeros_like(part))
                left[pl.ds(pl.multiple_of(i * PB, PB), PB), lo + j * SK : lo + (j + 1) * SK] = part.astype(bf16)
        return carry

    lax.fori_loop(0, ROWS // PB, left_rows, 0)

    @pl.when(r < RSRC)
    def _():
        for src_c in range(CSRC):
            @pl.when(c == src_c)
            def _():
                for i in range(1, NC):
                    t1(rem(c + i, NC), src_c, i).wait_send()
        for i in range(1, NR):
            for half in range(2):
                s1(half, rem(r + i, NR), r, i).wait_send()

    for src_c in range(CSRC):
        @pl.when(c == src_c)
        def _():
            for i in range(1, NC):
                b1(rem(c + i, NC), src_c, i).wait_send()
    for src_r, (hx, hz) in enumerate(homes):
        leg = 0 if src_r < 4 else 3

        @pl.when(r == src_r)
        def _():
            for n in range(3):
                t2(src_r, rem(r + 1, NR), leg + n).wait_send()

        @pl.when((z == hz) if src_r < 4 else (x == hx))
        def _():
            for n in range(3):
                t2(src_r, rem(r + 1, NR), 3 - leg + n).wait_send()
    for i in range(14):
        t3(c, 0, other, i).wait_send()
        b3(c, 0, other, i).wait_send()
    for half in range(2):
        for i in range(3):
            first(half, r, rem(r + 1, NR), i).wait_send()
        for i in range(24):
            second(half, r, 0, rem(r + 1, NR), i).wait_send()


def factors(b, s, t, core):
    vmem = pl.BlockSpec(memory_space=pltpu.VMEM)
    dma = pltpu.SemaphoreType.DMA
    bf16 = jnp.bfloat16
    return pl.pallas_call(
        factor_kernel,
        out_shape=(
            jax.ShapeDtypeStruct((ROWS, RANK), bf16),
            jax.ShapeDtypeStruct((BLOCKS, RANK, WIDE), bf16),
        ),
        in_specs=[vmem] * 4,
        out_specs=(vmem, vmem),
        scratch_shapes=[
            pltpu.VMEM((NC, TILE, RANK), bf16),
            pltpu.VMEM((NR, RSRC, 2 * SK, TILE), bf16),
            pltpu.VMEM((NC, RSRC, TR, RANK), bf16),
            pltpu.VMEM((RANK, RANK), jnp.float32),
            pltpu.VMEM((RANK, RANK), bf16),
            pltpu.VMEM((RANK, RANK), bf16),
            dma((3,)),
            dma((NC,)), dma((CSRC,)), dma((RSRC, 6)), dma((RSRC,)), dma((14,)), dma((NC, 2)),
            dma((NC,)), dma((CSRC,)), dma((14,)), dma((NC, 2)),
            dma((2, NR)), dma((2, RSRC)), dma((2, 3)), dma((2, NR)), dma((2, 24)), dma((2, NR, 2)),
        ],
        compiler_params=pltpu.CompilerParams(
            collective_id=1, has_side_effects=True, vmem_limit_bytes=34 * MIB
        ),
        name="panel_factors",
    )(b, s, t, core)


UR = 512


def update_kernel(left, right, grid, out_ref, obuf, osem):
    f32 = jnp.float32
    n = ROWS // UR

    def of_rows(i):
        return pl.ds(pl.multiple_of(i * UR, UR), UR)

    def store(i):
        return pltpu.make_async_copy(obuf.at[i], out_ref.at[of_rows(i)], osem.at[i])

    def rows(i, carry):
        def block(q, carry):
            cols = pl.ds(pl.multiple_of(q * WIDE, WIDE), WIDE)
            product = jnp.dot(left[of_rows(i), :], right[q], preferred_element_type=f32)
            obuf[i, :, cols] = (grid[of_rows(i), cols] - product).astype(jnp.bfloat16)
            return carry

        lax.fori_loop(0, BLOCKS, block, 0)
        store(i).start()
        return carry

    lax.fori_loop(0, n, rows, 0)
    for i in range(n):
        store(i).wait()


def update(left, right, grid):
    hbm = pl.BlockSpec(memory_space=pltpu.HBM)
    vmem = pl.BlockSpec(memory_space=pltpu.VMEM)
    n = ROWS // UR
    return pl.pallas_call(
        update_kernel,
        out_shape=jax.ShapeDtypeStruct((ROWS, COLS), jnp.bfloat16),
        in_specs=[vmem, vmem, vmem],
        out_specs=hbm,
        scratch_shapes=[pltpu.VMEM((n, UR, COLS), jnp.bfloat16), pltpu.SemaphoreType.DMA((n,))],
        compiler_params=pltpu.CompilerParams(vmem_limit_bytes=12 * MIB),
        name="panel_update",
    )(left, right, grid)


def shards(front, tiles, counts, dest_owner, dest_slot, omega, psi, core):
    owners = dest_owner[:, 0]
    strip = jnp.arange(ND, dtype=jnp.int32)
    same = owners[:, None] == owners[None, :]
    before = strip[None, :] < strip[:, None]
    ranks = jnp.sum((same & before).astype(jnp.int32), axis=1)
    valid = strip < counts[0]
    named = strip[None, :, None] == owners[None, None, :]
    hit = named & (ranks[None, None, :] == jnp.arange(CAP, dtype=jnp.int32)[:, None, None])
    idx = jnp.sum(jnp.where(hit, strip[None, None, :], 0), axis=2)
    slots = jnp.sum(jnp.where(hit & valid[None, None, :], dest_slot[None, None, :] + 1, 0), axis=2) - 1
    slots = jnp.pad(slots.T[:, None, :], ((0, 0), (0, 0), (0, TILE - CAP)))
    got, got_slots = exchange(idx, slots, tiles)
    grid, b, s, t = assemble(got_slots[:, 0, :], front, got, omega, psi)
    left, right = factors(b, s, t, core)
    return update(left, right, grid)


def solution(mesh):
    in_specs = (
        P("row", "col"),
        P(("row", "col"), None, None),
        P(("row", "col")),
        P(("row", "col"), None),
        P(("row", "col")),
        P(),
        P(),
        P(),
    )
    out_specs = P("row", "col")
    return jax.shard_map(shards, mesh=mesh, in_specs=in_specs, out_specs=out_specs, check_vma=False)
```

```python
import functools

import jax
import jax.numpy as jnp
from jax import lax
from jax.experimental import pallas as pl
from jax.experimental.pallas import tpu as pltpu
from jax.sharding import PartitionSpec as P

PB = 512
SK = 128
TILE = 128
PANELS = 10
CAP = 2
ND = 128
NR = 16
NC = 8
ROWS = 1024
COLS = 2048
RANK = PANELS * SK
RSRC = 5
CSRC = 3
MESH = pl.DeviceIdType.MESH
MIB = 2**20


def div(a, b):
    return lax.div(a, jnp.int32(b))


def rem(a, b):
    return lax.rem(a, jnp.int32(b))


def partner(me, step):
    j = rem(step * 31, 128)
    bit = lambda p: rem(div(j, 2**p), 2)
    dx = bit(0) * 2 + bit(3)
    dz = bit(5) * 2 + bit(4)
    dy = bit(6) * 2 + bit(2)
    dk = bit(1)
    x = rem(div(me, 32) + dx, 4)
    z = rem(div(me, 8) + dz, 4)
    y = rem(div(me, 2) + dy, 4)
    k = rem(me + dk, 2)
    return x * 32 + z * 8 + y * 2 + k


def exchange_kernel(
    idx_ref, slot_ref, tiles_ref, got_ref, gslot_ref, send, lsem, ssem, rsem, slot_ssem, slot_rsem
):
    me = lax.axis_index("row") * NC + lax.axis_index("col")
    barrier = pltpu.get_barrier_semaphore()

    def greet(step, carry):
        p = partner(me, step)
        pl.semaphore_signal(barrier, inc=1, device_id=(div(p, NC), rem(p, NC)), device_id_type=MESH)
        return carry

    lax.fori_loop(1, ND, greet, 0)
    own_slot = pltpu.make_async_copy(slot_ref.at[me], gslot_ref.at[me], lsem.at[0])
    own_slot.start()

    def pack(p):
        for k in range(CAP):
            send[p, k] = tiles_ref[idx_ref[k, p]]

    pack(me)
    own = pltpu.make_async_copy(send.at[me], got_ref.at[me], lsem.at[1])
    own.start()
    pl.semaphore_wait(barrier, ND - 1)

    def copies(p, landing):
        device = (div(p, NC), rem(p, NC))
        tile = pltpu.make_async_remote_copy(
            src_ref=send.at[p], dst_ref=got_ref.at[landing], send_sem=ssem.at[p], recv_sem=rsem.at[landing],
            device_id=device, device_id_type=MESH,
        )
        slot = pltpu.make_async_remote_copy(
            src_ref=slot_ref.at[p], dst_ref=gslot_ref.at[landing], send_sem=slot_ssem.at[p],
            recv_sem=slot_rsem.at[landing], device_id=device, device_id_type=MESH,
        )
        return tile, slot

    def post(step, carry):
        p = partner(me, step)
        pack(p)
        tile, slot = copies(p, me)
        tile.start()
        slot.start()
        return carry

    lax.fori_loop(1, ND, post, 0)

    def finish(step, carry):
        p = partner(me, step)
        tile, slot = copies(p, p)
        tile.wait()
        slot.wait()
        return carry

    lax.fori_loop(1, ND, finish, 0)
    own_slot.wait()
    own.wait()


def exchange(idx, slots, tiles):
    vmem = pl.BlockSpec(memory_space=pltpu.VMEM)
    return pl.pallas_call(
        exchange_kernel,
        out_shape=(
            jax.ShapeDtypeStruct((ND, CAP, TILE, TILE), jnp.bfloat16),
            jax.ShapeDtypeStruct((ND, 1, TILE), jnp.int32),
        ),
        in_specs=[pl.BlockSpec(memory_space=pltpu.SMEM), vmem, vmem],
        out_specs=(vmem, vmem),
        scratch_shapes=[
            pltpu.VMEM((ND, CAP, TILE, TILE), jnp.bfloat16),
            pltpu.SemaphoreType.DMA((2,)),
            pltpu.SemaphoreType.DMA((ND,)),
            pltpu.SemaphoreType.DMA((ND,)),
            pltpu.SemaphoreType.DMA((ND,)),
            pltpu.SemaphoreType.DMA((ND,)),
        ],
        compiler_params=pltpu.CompilerParams(
            collective_id=0, has_side_effects=True, vmem_limit_bytes=14 * MIB
        ),
        name="tile_exchange",
    )(idx, slots, tiles)


def assemble_kernel(
    gslot_ref, front_ref, got_ref, omega_ref, psi_ref, grid, b_ref, s_ref, t_ref, turned, slot_ref, sem
):
    r = lax.axis_index("row")
    c = lax.axis_index("col")

    turned[...] = gslot_ref[...].T[:8]
    to_scalar = pltpu.make_async_copy(turned, slot_ref, sem)
    to_scalar.start()

    def widen(i, carry):
        rows = pl.ds(pl.multiple_of(i * 64, 64), 64)
        grid[rows, :] = front_ref[rows, :].astype(jnp.float32)
        return carry

    lax.fori_loop(0, ROWS // 64, widen, 0)

    to_scalar.wait()

    def add_at(slot, source, k):
        rows = pl.ds(pl.multiple_of(div(slot, COLS // TILE) * TILE, TILE), TILE)
        cols = pl.ds(pl.multiple_of(rem(slot, COLS // TILE) * TILE, TILE), TILE)
        grid[rows, cols] += got_ref[source, k].astype(jnp.float32)

    def add(source, carry):
        slot = slot_ref[0, source]

        @pl.when(slot >= 0)
        def _():
            add_at(slot, source, 0)
            second = slot_ref[1, source]

            @pl.when(second >= 0)
            def _():
                add_at(second, source, 1)

        return carry

    lax.fori_loop(0, ND, add, 0, unroll=4)

    @pl.when(c < CSRC)
    def _():
        for k in range(4):
            block = grid[:, k * PB : (k + 1) * PB].astype(jnp.bfloat16)
            b_ref[:, k * SK : (k + 1) * SK] = jnp.dot(
                block, omega_ref[...], preferred_element_type=jnp.float32
            ).astype(jnp.bfloat16)

    @pl.when(r < RSRC)
    def _():
        psi_t = psi_ref[...].T
        for j in range(2):
            def cols_of(i, carry):
                cols = pl.ds(pl.multiple_of(i * 512, 512), 512)
                block = grid[j * PB : (j + 1) * PB, cols].astype(jnp.bfloat16)
                s_ref[j * SK : (j + 1) * SK, cols] = jnp.dot(
                    psi_t, block, preferred_element_type=jnp.float32
                ).astype(jnp.bfloat16)
                return carry

            lax.fori_loop(0, COLS // 512, cols_of, 0)

        @pl.when(c < CSRC)
        def _():
            for j in range(2):
                t_ref[j * SK : (j + 1) * SK, :] = jnp.dot(
                    psi_t, b_ref[j * PB : (j + 1) * PB, :], preferred_element_type=jnp.float32
                ).astype(jnp.bfloat16)


def assemble(slots, front, got, omega, psi):
    vmem = pl.BlockSpec(memory_space=pltpu.VMEM)
    return pl.pallas_call(
        assemble_kernel,
        out_shape=(
            jax.ShapeDtypeStruct((ROWS, COLS), jnp.float32),
            jax.ShapeDtypeStruct((ROWS, 4 * SK), jnp.bfloat16),
            jax.ShapeDtypeStruct((2 * SK, COLS), jnp.bfloat16),
            jax.ShapeDtypeStruct((2 * SK, 4 * SK), jnp.bfloat16),
        ),
        in_specs=[vmem] * 5,
        out_specs=(vmem, vmem, vmem, vmem),
        scratch_shapes=[
            pltpu.VMEM((8, TILE), jnp.int32),
            pltpu.SMEM((8, TILE), jnp.int32),
            pltpu.SemaphoreType.DMA,
        ],
        compiler_params=pltpu.CompilerParams(vmem_limit_bytes=6 * MIB),
        name="extend_add",
    )(slots, front, got, omega, psi)


TR = 2 * SK // NC
WIDE = 4 * TILE
BLOCKS = COLS // WIDE
STEPS = (1, 3, 2)
PLANE = (
    (1, 0), (3, 0), (0, 1), (2, 0), (1, 1), (3, 1), (0, 3), (2, 1),
    (1, 3), (3, 3), (0, 2), (2, 3), (1, 2), (3, 2), (2, 2),
)
LINE = ((1, 0), (3, 0), (1, 1), (3, 1), (2, 0), (2, 1), (0, 1))


def eliminate(tall, core, state, lmat, rmat, between):
    f32 = jnp.float32
    bf16 = jnp.bfloat16
    for cc in range(NC):
        for q in range(RSRC):
            lo = q * 2 * SK + cc * TR
            state[lo : lo + TR, :] = tall[cc, q].astype(f32)
    row = lax.broadcasted_iota(jnp.int32, (SK, SK), 0)
    col = lax.broadcasted_iota(jnp.int32, (SK, SK), 1)
    eye = jnp.where(row == col, 1.0, 0.0).astype(bf16)
    for s in range(PANELS):
        lo, hi = s * SK, (s + 1) * SK
        if s in between:
            between[s]()
        if s % 2 == 0:
            lmat[hi : hi + SK, lo:hi] = jnp.zeros((SK, SK), bf16)
            rmat[lo:hi, hi : hi + SK] = jnp.zeros((SK, SK), bf16)
        lmat[lo:hi, lo:hi] = core
        rmat[lo:hi, lo:hi] = eye
        if s:
            lmat[:lo, lo:hi] = jnp.dot(state[:lo, lo:hi].astype(bf16), core, preferred_element_type=f32).astype(bf16)
            rmat[lo:hi, :lo] = state[lo:hi, :lo].astype(bf16)
        if s == PANELS - 1:
            break
        below = jnp.dot(state[hi:, lo:hi].astype(bf16), core, preferred_element_type=f32).astype(bf16)
        beside = state[lo:hi, hi:].astype(bf16)
        state[hi:, hi:] -= jnp.dot(below, beside, preferred_element_type=f32)
        state[lo:hi, hi:] = -jnp.dot(core, beside, preferred_element_type=f32)
        state[hi:, lo:hi] = -below.astype(f32)
        if s:
            state[:lo, hi:] -= jnp.dot(lmat[:lo, lo:hi], beside, preferred_element_type=f32)
            state[hi:, :lo] -= jnp.dot(below, rmat[lo:hi, :lo], preferred_element_type=f32)


def factor_kernel(
    b_ref, s_ref, t_ref, core_ref, left, right,
    ball, sall, tall, state, lmat, rmat,
    lsem, t1s, t1r, t2s, t2r, t3s, t3r, bss, bsr, bas, bar, sss, ssr, s2s, s2r, s3s, s3r,
):
    r = lax.axis_index("row")
    c = lax.axis_index("col")
    x, z = div(r, 4), rem(r, 4)
    y, k = div(c, 2), rem(c, 2)
    other = y * 2 + (1 - k)
    f32 = jnp.float32
    bf16 = jnp.bfloat16

    barrier = pltpu.get_barrier_semaphore()
    for i in range(1, NR):
        pl.semaphore_signal(barrier, inc=1, device_id=(rem(r + i, NR), c), device_id_type=MESH)
    for i in range(1, NC):
        pl.semaphore_signal(barrier, inc=1, device_id=(r, rem(c + i, NC)), device_id_type=MESH)
    pl.semaphore_wait(barrier, NR - 1 + NC - 1)

    def remote(src, dst, send, recv, device):
        return pltpu.make_async_remote_copy(
            src_ref=src, dst_ref=dst, send_sem=send, recv_sem=recv, device_id=device, device_id_type=MESH
        )

    widths = [4 * SK, 4 * SK, 2 * SK]

    def t1(cc, src_c, sem):
        w = widths[src_c]
        return remote(
            t_ref.at[pl.ds(pl.multiple_of(cc * TR, TR), TR), pl.ds(0, w)],
            tall.at[cc, r, :, pl.ds(src_c * 4 * SK, w)],
            t1s.at[sem], t1r.at[src_c], (r, cc),
        )

    def b1(cc, src_c, sem):
        w = widths[src_c]
        return remote(
            b_ref.at[pl.ds(pl.multiple_of(cc * TILE, TILE), TILE), pl.ds(0, w)],
            ball.at[cc, :, pl.ds(src_c * 4 * SK, w)],
            bss.at[sem], bsr.at[src_c], (r, cc),
        )

    def s1(half, rr, src_r, sem):
        rows = pl.ds(half * SK, SK)
        return remote(
            s_ref.at[rows, pl.ds(pl.multiple_of(rr * TILE, TILE), TILE)], sall.at[rr, src_r, rows, :],
            sss.at[half, sem], ssr.at[half, src_r], (rr, c),
        )

    def own_t(src_c):
        w = widths[src_c]
        return pltpu.make_async_copy(
            t_ref.at[pl.ds(pl.multiple_of(c * TR, TR), TR), pl.ds(0, w)],
            tall.at[c, r, :, pl.ds(src_c * 4 * SK, w)], lsem.at[0],
        )

    def own_b(src_c):
        w = widths[src_c]
        return pltpu.make_async_copy(
            b_ref.at[pl.ds(pl.multiple_of(c * TILE, TILE), TILE), pl.ds(0, w)],
            ball.at[c, :, pl.ds(src_c * 4 * SK, w)], lsem.at[1],
        )

    def own_s():
        return pltpu.make_async_copy(
            s_ref.at[:, pl.ds(pl.multiple_of(r * TILE, TILE), TILE)], sall.at[r, r], lsem.at[2]
        )

    @pl.when(r < RSRC)
    def _():
        for src_c in range(CSRC):
            @pl.when(c == src_c)
            def _():
                own_t(src_c).start()
                for i, (dy, dk) in enumerate(LINE):
                    t1(rem(y + dy, 4) * 2 + rem(k + dk, 2), src_c, 1 + i).start()

    for src_c in range(CSRC):
        @pl.when(c == src_c)
        def _():
            own_b(src_c).start()
            for i, (dy, dk) in enumerate(LINE):
                b1(rem(y + dy, 4) * 2 + rem(k + dk, 2), src_c, 1 + i).start()

    homes = [(0, 0), (0, 1), (0, 2), (0, 3), (1, 0)]

    def t2(src_r, rr, sem):
        return remote(tall.at[c, src_r], tall.at[c, src_r], t2s.at[src_r, sem], t2r.at[src_r], (rr, c))

    @pl.when(r < RSRC)
    def _():
        for src_c in range(CSRC):
            @pl.when(c != src_c)
            def _():
                t1(c, src_c, 0).wait_recv()

            @pl.when(c == src_c)
            def _():
                own_t(src_c).wait()

    for src_r, (hx, hz) in enumerate(homes):
        @pl.when(r == src_r)
        def _():
            for n, d in enumerate(STEPS):
                t2(src_r, rem(x + d, 4) * 4 + z, n).start()
                t2(src_r, x * 4 + rem(z + d, 4), 3 + n).start()

    axes = (("x", "z"), ("z", "x"))

    @pl.when(r < RSRC)
    def _():
        own_s().start()
        for half in range(2):
            for i, (dx, dz) in enumerate(PLANE):
                s1(half, rem(x + dx, 4) * 4 + rem(z + dz, 4), r, 1 + i).start()

    for src_r, (hx, hz) in enumerate(homes):
        if src_r < 4:
            @pl.when((z == hz) & (x != hx))
            def _():
                t2(src_r, r, 0).wait_recv()
                for n, d in enumerate(STEPS):
                    t2(src_r, x * 4 + rem(z + d, 4), 3 + n).start()
        else:
            @pl.when((x == hx) & (z != hz))
            def _():
                t2(src_r, r, 0).wait_recv()
                for n, d in enumerate(STEPS):
                    t2(src_r, rem(x + d, 4) * 4 + z, n).start()

    up = rem(y + 1, 4) * 2 + k
    down = rem(y + 3, 4) * 2 + k
    far = rem(y + 2, 4) * 2 + k

    def t3(piece, h, cc, sem):
        part = tall.at[piece, :, pl.ds(h * (TR // 2), TR // 2), :]
        return remote(part, part, t3s.at[sem], t3r.at[piece, h], (r, cc))

    def b3(piece, h, cc, sem):
        part = ball.at[piece, pl.ds(h * (TILE // 2), TILE // 2), :]
        return remote(part, part, bas.at[sem], bar.at[piece, h], (r, cc))

    def post_own(copy):
        copy(c, 0, up, 0).start()
        copy(c, 1, down, 1).start()
        copy(c, 1, up, 2).start()
        copy(c, 0, down, 3).start()
        copy(c, 0, other, 4).start()
        copy(c, 1, other, 5).start()

    def post_relays(copy):
        copy(down, 0, c, 0).wait_recv()
        copy(down, 0, up, 6).start()
        copy(down, 0, other, 7).start()
        copy(up, 1, c, 0).wait_recv()
        copy(up, 1, down, 8).start()
        copy(up, 1, other, 9).start()
        copy(down, 1, c, 0).wait_recv()
        copy(down, 1, other, 10).start()
        copy(up, 0, c, 0).wait_recv()
        copy(up, 0, other, 11).start()

    def post_far(copy):
        for h in range(2):
            copy(far, h, c, 0).wait_recv()
            copy(far, h, other, 12 + h).start()

    def wait_other(copy):
        for yy in range(4):
            for h in range(2):
                copy(yy * 2 + (1 - k), h, c, 0).wait_recv()

    for src_c in range(CSRC):
        @pl.when(c != src_c)
        def _():
            b1(c, src_c, 0).wait_recv()

        @pl.when(c == src_c)
        def _():
            own_b(src_c).wait()
    post_own(b3)

    for src_r, (hx, hz) in enumerate(homes):
        @pl.when((z != hz) if src_r < 4 else (x != hx))
        def _():
            t2(src_r, r, 0).wait_recv()
    post_own(t3)

    def along(axis, d):
        if axis == "x":
            return rem(x + d, 4) * 4 + z
        return x * 4 + rem(z + d, 4)

    def first(half, piece, rr, sem):
        part = sall.at[piece, :, pl.ds(half * SK, SK), :]
        return remote(part, part, s2s.at[half, sem], s2r.at[half, piece], (rr, c))

    def second(half, piece, q, rr, sem):
        part = sall.at[piece, :, pl.ds(half * SK + q * (SK // 2), SK // 2), :]
        return remote(part, part, s3s.at[half, sem], s3r.at[half, piece, q], (rr, c))

    def post_second(half, piece, m):
        plus = along(axes[half][1], 1)
        minus = along(axes[half][1], 3)
        second(half, piece, 0, plus, 6 * m).start()
        second(half, piece, 1, minus, 6 * m + 1).start()
        second(half, piece, 1, plus, 6 * m + 2).start()
        second(half, piece, 0, minus, 6 * m + 3).start()

    def relay_second(half, d, m):
        for q, side, onward in ((0, 3, 1), (1, 1, 3)):
            if axes[half][0] == "x":
                piece = rem(x + d, 4) * 4 + rem(z + side, 4)
            else:
                piece = rem(x + side, 4) * 4 + rem(z + d, 4)
            second(half, piece, q, r, 0).wait_recv()
            second(half, piece, q, along(axes[half][1], onward), 6 * m + 4 + q).start()

    def settle(half, piece, distance):
        @pl.when(distance != 3)
        def _():
            second(half, piece, 0, r, 0).wait_recv()

        @pl.when(distance != 1)
        def _():
            second(half, piece, 1, r, 0).wait_recv()

    for half in range(2):
        for src_r in range(RSRC):
            @pl.when(r != src_r)
            def _():
                s1(half, r, src_r, 0).wait_recv()

            if half == 0:
                @pl.when(r == src_r)
                def _():
                    own_s().wait()
        for n, d in enumerate(STEPS):
            first(half, r, along(axes[half][0], d), n).start()
        post_second(half, r, 0)

    post_relays(b3)
    for half in range(2):
        relay_second(half, 0, 0)
    for m, d in enumerate(STEPS):
        for half in range(2):
            piece = along(axes[half][0], d)
            first(half, piece, r, 0).wait_recv()
            post_second(half, piece, 1 + m)
    post_relays(t3)
    post_far(b3)
    for half in range(2):
        relay_second(half, STEPS[0], 1)
    post_far(t3)
    wait_other(t3)

    def relay_both(m):
        for half in range(2):
            relay_second(half, STEPS[m], 1 + m)

    core = core_ref[...]
    eliminate(tall, core, state, lmat, rmat, {1: lambda: relay_both(1), 5: lambda: relay_both(2)})

    wait_other(b3)

    def left_rows(i, carry):
        panel = r * (ROWS // PB) + i
        block = jnp.concatenate([ball[i * 4 + h] for h in range(4)], axis=0)
        for q in range(RSRC):
            lo, hi = q * 2 * SK, (q + 1) * 2 * SK
            out = jnp.dot(block[:, :hi], lmat[:hi, lo:hi], preferred_element_type=f32)
            for j in range(2):
                part = out[:, j * SK : (j + 1) * SK]
                part = jnp.where(2 * q + j < panel, part, jnp.zeros_like(part))
                left[pl.ds(pl.multiple_of(i * PB, PB), PB), lo + j * SK : lo + (j + 1) * SK] = part.astype(bf16)
        return carry

    lax.fori_loop(0, ROWS // PB, left_rows, 0)

    def right_block(i, carry):
        dx = i + div(i, 2) - 2 * div(i, 3)
        xx = rem(x + dx, 4)
        for zz in range(4):
            piece = xx * 4 + zz
            dz = rem(zz - z + 4, 4)

            @pl.when(dz != 0)
            def _():
                settle(0, piece, dz)

            @pl.when(dx != 0)
            def _():
                settle(1, piece, dx)

        block = jnp.concatenate([sall[xx * 4 + h].reshape(RANK, TILE) for h in range(4)], axis=1)
        panel = c * (COLS // PB) + xx
        for q in range(RSRC):
            lo, hi = q * 2 * SK, (q + 1) * 2 * SK
            out = jnp.dot(rmat[lo:hi, :hi], block[:hi], preferred_element_type=f32)
            for j in range(2):
                part = out[j * SK : (j + 1) * SK]
                part = jnp.where(2 * q + j < panel, part, jnp.zeros_like(part))
                right[xx, lo + j * SK : lo + (j + 1) * SK, :] = part.astype(bf16)
        return carry

    lax.fori_loop(0, BLOCKS, right_block, 0)

    @pl.when(r < RSRC)
    def _():
        for src_c in range(CSRC):
            @pl.when(c == src_c)
            def _():
                for i in range(1, NC):
                    t1(rem(c + i, NC), src_c, i).wait_send()
        for i in range(1, NR):
            for half in range(2):
                s1(half, rem(r + i, NR), r, i).wait_send()

    for src_c in range(CSRC):
        @pl.when(c == src_c)
        def _():
            for i in range(1, NC):
                b1(rem(c + i, NC), src_c, i).wait_send()
    for src_r, (hx, hz) in enumerate(homes):
        leg = 0 if src_r < 4 else 3

        @pl.when(r == src_r)
        def _():
            for n in range(3):
                t2(src_r, rem(r + 1, NR), leg + n).wait_send()

        @pl.when((z == hz) if src_r < 4 else (x == hx))
        def _():
            for n in range(3):
                t2(src_r, rem(r + 1, NR), 3 - leg + n).wait_send()
    for i in range(14):
        t3(c, 0, other, i).wait_send()
        b3(c, 0, other, i).wait_send()
    for half in range(2):
        for i in range(3):
            first(half, r, rem(r + 1, NR), i).wait_send()
        for i in range(24):
            second(half, r, 0, rem(r + 1, NR), i).wait_send()


def factors(b, s, t, core):
    vmem = pl.BlockSpec(memory_space=pltpu.VMEM)
    dma = pltpu.SemaphoreType.DMA
    bf16 = jnp.bfloat16
    return pl.pallas_call(
        factor_kernel,
        out_shape=(
            jax.ShapeDtypeStruct((ROWS, RANK), bf16),
            jax.ShapeDtypeStruct((BLOCKS, RANK, WIDE), bf16),
        ),
        in_specs=[vmem] * 4,
        out_specs=(vmem, vmem),
        scratch_shapes=[
            pltpu.VMEM((NC, TILE, RANK), bf16),
            pltpu.VMEM((NR, RSRC, 2 * SK, TILE), bf16),
            pltpu.VMEM((NC, RSRC, TR, RANK), bf16),
            pltpu.VMEM((RANK, RANK), jnp.float32),
            pltpu.VMEM((RANK, RANK), bf16),
            pltpu.VMEM((RANK, RANK), bf16),
            dma((3,)),
            dma((NC,)), dma((CSRC,)), dma((RSRC, 6)), dma((RSRC,)), dma((14,)), dma((NC, 2)),
            dma((NC,)), dma((CSRC,)), dma((14,)), dma((NC, 2)),
            dma((2, NR)), dma((2, RSRC)), dma((2, 3)), dma((2, NR)), dma((2, 24)), dma((2, NR, 2)),
        ],
        compiler_params=pltpu.CompilerParams(
            collective_id=1, has_side_effects=True, vmem_limit_bytes=34 * MIB
        ),
        name="panel_factors",
    )(b, s, t, core)


UR = 512


def update_kernel(left, right, grid, out_ref, obuf, osem):
    f32 = jnp.float32
    n = ROWS // UR

    def of_rows(i):
        return pl.ds(pl.multiple_of(i * UR, UR), UR)

    def store(i, q):
        cols = pl.ds(pl.multiple_of(q * WIDE, WIDE), WIDE)
        return pltpu.make_async_copy(obuf.at[i, :, cols], out_ref.at[of_rows(i), cols], osem.at[i, q])

    def rows(i, carry):
        def block(q, carry):
            cols = pl.ds(pl.multiple_of(q * WIDE, WIDE), WIDE)
            product = jnp.dot(left[of_rows(i), :], right[q], preferred_element_type=f32)
            obuf[i, :, cols] = (grid[of_rows(i), cols] - product).astype(jnp.bfloat16)
            store(i, q).start()
            return carry

        lax.fori_loop(0, BLOCKS, block, 0)
        return carry

    lax.fori_loop(0, n, rows, 0)
    for i in range(n):
        for q in range(BLOCKS):
            store(i, q).wait()


def update(left, right, grid):
    hbm = pl.BlockSpec(memory_space=pltpu.HBM)
    vmem = pl.BlockSpec(memory_space=pltpu.VMEM)
    n = ROWS // UR
    return pl.pallas_call(
        update_kernel,
        out_shape=jax.ShapeDtypeStruct((ROWS, COLS), jnp.bfloat16),
        in_specs=[vmem, vmem, vmem],
        out_specs=hbm,
        scratch_shapes=[pltpu.VMEM((n, UR, COLS), jnp.bfloat16), pltpu.SemaphoreType.DMA((n, BLOCKS))],
        compiler_params=pltpu.CompilerParams(vmem_limit_bytes=12 * MIB),
        name="panel_update",
    )(left, right, grid)


def shards(front, tiles, counts, dest_owner, dest_slot, omega, psi, core):
    owners = dest_owner[:, 0]
    strip = jnp.arange(ND, dtype=jnp.int32)
    same = owners[:, None] == owners[None, :]
    before = strip[None, :] < strip[:, None]
    ranks = jnp.sum((same & before).astype(jnp.int32), axis=1)
    valid = strip < counts[0]
    named = strip[None, :, None] == owners[None, None, :]
    hit = named & (ranks[None, None, :] == jnp.arange(CAP, dtype=jnp.int32)[:, None, None])
    idx = jnp.sum(jnp.where(hit, strip[None, None, :], 0), axis=2)
    slots = jnp.sum(jnp.where(hit & valid[None, None, :], dest_slot[None, None, :] + 1, 0), axis=2) - 1
    slots = jnp.pad(slots.T[:, None, :], ((0, 0), (0, 0), (0, TILE - CAP)))
    got, got_slots = exchange(idx, slots, tiles)
    grid, b, s, t = assemble(got_slots[:, 0, :], front, got, omega, psi)
    left, right = factors(b, s, t, core)
    return update(left, right, grid)


def solution(mesh):
    in_specs = (
        P("row", "col"),
        P(("row", "col"), None, None),
        P(("row", "col")),
        P(("row", "col"), None),
        P(("row", "col")),
        P(),
        P(),
        P(),
    )
    out_specs = P("row", "col")
    return jax.shard_map(shards, mesh=mesh, in_specs=in_specs, out_specs=out_specs, check_vma=False)
```

```python
import functools

import jax
import jax.numpy as jnp
from jax import lax
from jax.experimental import pallas as pl
from jax.experimental.pallas import tpu as pltpu
from jax.sharding import PartitionSpec as P

PB = 512
SK = 128
TILE = 128
PANELS = 10
CAP = 2
ND = 128
NR = 16
NC = 8
ROWS = 1024
COLS = 2048
RANK = PANELS * SK
RSRC = 5
CSRC = 3
MESH = pl.DeviceIdType.MESH
MIB = 2**20


def div(a, b):
    return lax.div(a, jnp.int32(b))


def rem(a, b):
    return lax.rem(a, jnp.int32(b))


def partner(me, step):
    j = rem(step * 31, 128)
    bit = lambda p: rem(div(j, 2**p), 2)
    dx = bit(0) * 2 + bit(3)
    dz = bit(5) * 2 + bit(4)
    dy = bit(6) * 2 + bit(2)
    dk = bit(1)
    x = rem(div(me, 32) + dx, 4)
    z = rem(div(me, 8) + dz, 4)
    y = rem(div(me, 2) + dy, 4)
    k = rem(me + dk, 2)
    return x * 32 + z * 8 + y * 2 + k


def exchange_kernel(
    idx_ref, slot_ref, tiles_ref, got_ref, gslot_ref, send, lsem, ssem, rsem, slot_ssem, slot_rsem
):
    me = lax.axis_index("row") * NC + lax.axis_index("col")
    barrier = pltpu.get_barrier_semaphore()

    def greet(step, carry):
        p = partner(me, step)
        pl.semaphore_signal(barrier, inc=1, device_id=(div(p, NC), rem(p, NC)), device_id_type=MESH)
        return carry

    lax.fori_loop(1, ND, greet, 0)
    own_slot = pltpu.make_async_copy(slot_ref.at[me], gslot_ref.at[me], lsem.at[0])
    own_slot.start()

    def pack(p):
        for k in range(CAP):
            send[p, k] = tiles_ref[idx_ref[k, p]]

    pack(me)
    own = pltpu.make_async_copy(send.at[me], got_ref.at[me], lsem.at[1])
    own.start()
    pl.semaphore_wait(barrier, ND - 1)

    def copies(p, landing):
        device = (div(p, NC), rem(p, NC))
        tile = pltpu.make_async_remote_copy(
            src_ref=send.at[p], dst_ref=got_ref.at[landing], send_sem=ssem.at[p], recv_sem=rsem.at[landing],
            device_id=device, device_id_type=MESH,
        )
        slot = pltpu.make_async_remote_copy(
            src_ref=slot_ref.at[p], dst_ref=gslot_ref.at[landing], send_sem=slot_ssem.at[p],
            recv_sem=slot_rsem.at[landing], device_id=device, device_id_type=MESH,
        )
        return tile, slot

    def post(step, carry):
        p = partner(me, step)
        pack(p)
        tile, slot = copies(p, me)
        tile.start()
        slot.start()
        return carry

    lax.fori_loop(1, ND, post, 0)

    def finish(step, carry):
        p = partner(me, step)
        tile, slot = copies(p, p)
        tile.wait()
        slot.wait()
        return carry

    lax.fori_loop(1, ND, finish, 0)
    own_slot.wait()
    own.wait()


def exchange(idx, slots, tiles):
    vmem = pl.BlockSpec(memory_space=pltpu.VMEM)
    return pl.pallas_call(
        exchange_kernel,
        out_shape=(
            jax.ShapeDtypeStruct((ND, CAP, TILE, TILE), jnp.bfloat16),
            jax.ShapeDtypeStruct((ND, 1, TILE), jnp.int32),
        ),
        in_specs=[pl.BlockSpec(memory_space=pltpu.SMEM), vmem, vmem],
        out_specs=(vmem, vmem),
        scratch_shapes=[
            pltpu.VMEM((ND, CAP, TILE, TILE), jnp.bfloat16),
            pltpu.SemaphoreType.DMA((2,)),
            pltpu.SemaphoreType.DMA((ND,)),
            pltpu.SemaphoreType.DMA((ND,)),
            pltpu.SemaphoreType.DMA((ND,)),
            pltpu.SemaphoreType.DMA((ND,)),
        ],
        compiler_params=pltpu.CompilerParams(
            collective_id=0, has_side_effects=True, vmem_limit_bytes=14 * MIB
        ),
        name="tile_exchange",
    )(idx, slots, tiles)


def assemble_kernel(
    gslot_ref, front_ref, got_ref, omega_ref, psi_ref, grid, b_ref, s_ref, t_ref, turned, slot_ref, sem
):
    r = lax.axis_index("row")
    c = lax.axis_index("col")

    turned[...] = gslot_ref[...].T[:8]
    to_scalar = pltpu.make_async_copy(turned, slot_ref, sem)
    to_scalar.start()

    def widen(i, carry):
        rows = pl.ds(pl.multiple_of(i * 64, 64), 64)
        grid[rows, :] = front_ref[rows, :].astype(jnp.float32)
        return carry

    lax.fori_loop(0, ROWS // 64, widen, 0)

    to_scalar.wait()

    def add_at(slot, source, k):
        rows = pl.ds(pl.multiple_of(div(slot, COLS // TILE) * TILE, TILE), TILE)
        cols = pl.ds(pl.multiple_of(rem(slot, COLS // TILE) * TILE, TILE), TILE)
        grid[rows, cols] += got_ref[source, k].astype(jnp.float32)

    def add(source, carry):
        slot = slot_ref[0, source]

        @pl.when(slot >= 0)
        def _():
            add_at(slot, source, 0)
            second = slot_ref[1, source]

            @pl.when(second >= 0)
            def _():
                add_at(second, source, 1)

        return carry

    lax.fori_loop(0, ND, add, 0, unroll=4)

    @pl.when(c < CSRC)
    def _():
        for k in range(4):
            block = grid[:, k * PB : (k + 1) * PB].astype(jnp.bfloat16)
            b_ref[:, k * SK : (k + 1) * SK] = jnp.dot(
                block, omega_ref[...], preferred_element_type=jnp.float32
            ).astype(jnp.bfloat16)

    @pl.when(r < RSRC)
    def _():
        psi_t = psi_ref[...].T
        for j in range(2):
            def cols_of(i, carry):
                cols = pl.ds(pl.multiple_of(i * 512, 512), 512)
                block = grid[j * PB : (j + 1) * PB, cols].astype(jnp.bfloat16)
                s_ref[j * SK : (j + 1) * SK, cols] = jnp.dot(
                    psi_t, block, preferred_element_type=jnp.float32
                ).astype(jnp.bfloat16)
                return carry

            lax.fori_loop(0, COLS // 512, cols_of, 0)

        @pl.when(c < CSRC)
        def _():
            for j in range(2):
                t_ref[j * SK : (j + 1) * SK, :] = jnp.dot(
                    psi_t, b_ref[j * PB : (j + 1) * PB, :], preferred_element_type=jnp.float32
                ).astype(jnp.bfloat16)


def assemble(slots, front, got, omega, psi):
    vmem = pl.BlockSpec(memory_space=pltpu.VMEM)
    return pl.pallas_call(
        assemble_kernel,
        out_shape=(
            jax.ShapeDtypeStruct((ROWS, COLS), jnp.float32),
            jax.ShapeDtypeStruct((ROWS, 4 * SK), jnp.bfloat16),
            jax.ShapeDtypeStruct((2 * SK, COLS), jnp.bfloat16),
            jax.ShapeDtypeStruct((2 * SK, 4 * SK), jnp.bfloat16),
        ),
        in_specs=[vmem] * 5,
        out_specs=(vmem, vmem, vmem, vmem),
        scratch_shapes=[
            pltpu.VMEM((8, TILE), jnp.int32),
            pltpu.SMEM((8, TILE), jnp.int32),
            pltpu.SemaphoreType.DMA,
        ],
        compiler_params=pltpu.CompilerParams(vmem_limit_bytes=6 * MIB),
        name="extend_add",
    )(slots, front, got, omega, psi)


TR = 2 * SK // NC
WIDE = 4 * TILE
BLOCKS = COLS // WIDE
STEPS = (1, 3, 2)
PLANE = (
    (1, 0), (3, 0), (0, 1), (2, 0), (1, 1), (3, 1), (0, 3), (2, 1),
    (1, 3), (3, 3), (0, 2), (2, 3), (1, 2), (3, 2), (2, 2),
)
LINE = ((1, 0), (3, 0), (1, 1), (3, 1), (2, 0), (2, 1), (0, 1))


def eliminate(tall, core, state, lmat, rmat, between):
    f32 = jnp.float32
    bf16 = jnp.bfloat16
    for cc in range(NC):
        for q in range(RSRC):
            lo = q * 2 * SK + cc * TR
            state[lo : lo + TR, :] = tall[cc, q].astype(f32)
    row = lax.broadcasted_iota(jnp.int32, (SK, SK), 0)
    col = lax.broadcasted_iota(jnp.int32, (SK, SK), 1)
    eye = jnp.where(row == col, 1.0, 0.0).astype(bf16)
    for s in range(PANELS):
        lo, hi = s * SK, (s + 1) * SK
        if s in between:
            between[s]()
        if s % 2 == 0:
            lmat[hi : hi + SK, lo:hi] = jnp.zeros((SK, SK), bf16)
            rmat[lo:hi, hi : hi + SK] = jnp.zeros((SK, SK), bf16)
        lmat[lo:hi, lo:hi] = core
        rmat[lo:hi, lo:hi] = eye
        if s:
            lmat[:lo, lo:hi] = jnp.dot(state[:lo, lo:hi].astype(bf16), core, preferred_element_type=f32).astype(bf16)
            rmat[lo:hi, :lo] = state[lo:hi, :lo].astype(bf16)
        if s == PANELS - 1:
            break
        below = jnp.dot(state[hi:, lo:hi].astype(bf16), core, preferred_element_type=f32).astype(bf16)
        beside = state[lo:hi, hi:].astype(bf16)
        state[hi:, hi:] -= jnp.dot(below, beside, preferred_element_type=f32)
        state[lo:hi, hi:] = -jnp.dot(core, beside, preferred_element_type=f32)
        state[hi:, lo:hi] = -below.astype(f32)
        if s:
            state[:lo, hi:] -= jnp.dot(lmat[:lo, lo:hi], beside, preferred_element_type=f32)
            state[hi:, :lo] -= jnp.dot(below, rmat[lo:hi, :lo], preferred_element_type=f32)


def factor_kernel(
    b_ref, s_ref, t_ref, core_ref, left, right,
    ball, sall, tall, state, lmat, rmat,
    lsem, t1s, t1r, t2s, t2r, t3s, t3r, bss, bsr, bas, bar, sss, ssr, s2s, s2r, s3s, s3r,
):
    r = lax.axis_index("row")
    c = lax.axis_index("col")
    x, z = div(r, 4), rem(r, 4)
    y, k = div(c, 2), rem(c, 2)
    other = y * 2 + (1 - k)
    f32 = jnp.float32
    bf16 = jnp.bfloat16

    barrier = pltpu.get_barrier_semaphore()
    for i in range(1, NR):
        pl.semaphore_signal(barrier, inc=1, device_id=(rem(r + i, NR), c), device_id_type=MESH)
    for i in range(1, NC):
        pl.semaphore_signal(barrier, inc=1, device_id=(r, rem(c + i, NC)), device_id_type=MESH)
    pl.semaphore_wait(barrier, NR - 1 + NC - 1)

    def remote(src, dst, send, recv, device):
        return pltpu.make_async_remote_copy(
            src_ref=src, dst_ref=dst, send_sem=send, recv_sem=recv, device_id=device, device_id_type=MESH
        )

    widths = [4 * SK, 4 * SK, 2 * SK]

    def t1(cc, src_c, sem):
        w = widths[src_c]
        return remote(
            t_ref.at[pl.ds(pl.multiple_of(cc * TR, TR), TR), pl.ds(0, w)],
            tall.at[cc, r, :, pl.ds(src_c * 4 * SK, w)],
            t1s.at[sem], t1r.at[src_c], (r, cc),
        )

    def b1(cc, src_c, sem):
        w = widths[src_c]
        return remote(
            b_ref.at[pl.ds(pl.multiple_of(cc * TILE, TILE), TILE), pl.ds(0, w)],
            ball.at[cc, :, pl.ds(src_c * 4 * SK, w)],
            bss.at[sem], bsr.at[src_c], (r, cc),
        )

    def s1(half, rr, src_r, sem):
        rows = pl.ds(half * SK, SK)
        return remote(
            s_ref.at[rows, pl.ds(pl.multiple_of(rr * TILE, TILE), TILE)], sall.at[rr, src_r, rows, :],
            sss.at[half, sem], ssr.at[half, src_r], (rr, c),
        )

    def own_t(src_c):
        w = widths[src_c]
        return pltpu.make_async_copy(
            t_ref.at[pl.ds(pl.multiple_of(c * TR, TR), TR), pl.ds(0, w)],
            tall.at[c, r, :, pl.ds(src_c * 4 * SK, w)], lsem.at[0],
        )

    def own_b(src_c):
        w = widths[src_c]
        return pltpu.make_async_copy(
            b_ref.at[pl.ds(pl.multiple_of(c * TILE, TILE), TILE), pl.ds(0, w)],
            ball.at[c, :, pl.ds(src_c * 4 * SK, w)], lsem.at[1],
        )

    def own_s():
        return pltpu.make_async_copy(
            s_ref.at[:, pl.ds(pl.multiple_of(r * TILE, TILE), TILE)], sall.at[r, r], lsem.at[2]
        )

    @pl.when(r < RSRC)
    def _():
        for src_c in range(CSRC):
            @pl.when(c == src_c)
            def _():
                own_t(src_c).start()
                for i, (dy, dk) in enumerate(LINE):
                    t1(rem(y + dy, 4) * 2 + rem(k + dk, 2), src_c, 1 + i).start()

    for src_c in range(CSRC):
        @pl.when(c == src_c)
        def _():
            own_b(src_c).start()
            for i, (dy, dk) in enumerate(LINE):
                b1(rem(y + dy, 4) * 2 + rem(k + dk, 2), src_c, 1 + i).start()

    homes = [(0, 0), (0, 1), (0, 2), (0, 3), (1, 0)]

    def t2(src_r, rr, sem):
        return remote(tall.at[c, src_r], tall.at[c, src_r], t2s.at[src_r, sem], t2r.at[src_r], (rr, c))

    @pl.when(r < RSRC)
    def _():
        for src_c in range(CSRC):
            @pl.when(c != src_c)
            def _():
                t1(c, src_c, 0).wait_recv()

            @pl.when(c == src_c)
            def _():
                own_t(src_c).wait()

    for src_r, (hx, hz) in enumerate(homes):
        @pl.when(r == src_r)
        def _():
            for n, d in enumerate(STEPS):
                t2(src_r, rem(x + d, 4) * 4 + z, n).start()
                t2(src_r, x * 4 + rem(z + d, 4), 3 + n).start()

    axes = (("x", "z"), ("z", "x"))

    @pl.when(r < RSRC)
    def _():
        own_s().start()
        for half in range(2):
            for i, (dx, dz) in enumerate(PLANE):
                s1(half, rem(x + dx, 4) * 4 + rem(z + dz, 4), r, 1 + i).start()

    for src_r, (hx, hz) in enumerate(homes):
        if src_r < 4:
            @pl.when((z == hz) & (x != hx))
            def _():
                t2(src_r, r, 0).wait_recv()
                for n, d in enumerate(STEPS):
                    t2(src_r, x * 4 + rem(z + d, 4), 3 + n).start()
        else:
            @pl.when((x == hx) & (z != hz))
            def _():
                t2(src_r, r, 0).wait_recv()
                for n, d in enumerate(STEPS):
                    t2(src_r, rem(x + d, 4) * 4 + z, n).start()

    up = rem(y + 1, 4) * 2 + k
    down = rem(y + 3, 4) * 2 + k
    far = rem(y + 2, 4) * 2 + k

    def t3(piece, h, cc, sem):
        part = tall.at[piece, :, pl.ds(h * (TR // 2), TR // 2), :]
        return remote(part, part, t3s.at[sem], t3r.at[piece, h], (r, cc))

    def b3(piece, h, cc, sem):
        part = ball.at[piece, pl.ds(h * (TILE // 2), TILE // 2), :]
        return remote(part, part, bas.at[sem], bar.at[piece, h], (r, cc))

    def post_own(copy):
        copy(c, 0, up, 0).start()
        copy(c, 1, down, 1).start()
        copy(c, 1, up, 2).start()
        copy(c, 0, down, 3).start()
        copy(c, 0, other, 4).start()
        copy(c, 1, other, 5).start()

    def post_relays(copy):
        copy(down, 0, c, 0).wait_recv()
        copy(down, 0, up, 6).start()
        copy(down, 0, other, 7).start()
        copy(up, 1, c, 0).wait_recv()
        copy(up, 1, down, 8).start()
        copy(up, 1, other, 9).start()
        copy(down, 1, c, 0).wait_recv()
        copy(down, 1, other, 10).start()
        copy(up, 0, c, 0).wait_recv()
        copy(up, 0, other, 11).start()

    def post_far(copy):
        for h in range(2):
            copy(far, h, c, 0).wait_recv()
            copy(far, h, other, 12 + h).start()

    def wait_other(copy):
        for yy in range(4):
            for h in range(2):
                copy(yy * 2 + (1 - k), h, c, 0).wait_recv()

    for src_c in range(CSRC):
        @pl.when(c != src_c)
        def _():
            b1(c, src_c, 0).wait_recv()

        @pl.when(c == src_c)
        def _():
            own_b(src_c).wait()
    post_own(b3)

    for src_r, (hx, hz) in enumerate(homes):
        @pl.when((z != hz) if src_r < 4 else (x != hx))
        def _():
            t2(src_r, r, 0).wait_recv()
    post_own(t3)

    def along(axis, d):
        if axis == "x":
            return rem(x + d, 4) * 4 + z
        return x * 4 + rem(z + d, 4)

    def first(half, piece, rr, sem):
        part = sall.at[piece, :, pl.ds(half * SK, SK), :]
        return remote(part, part, s2s.at[half, sem], s2r.at[half, piece], (rr, c))

    def second(half, piece, q, rr, sem):
        part = sall.at[piece, :, pl.ds(half * SK + q * (SK // 2), SK // 2), :]
        return remote(part, part, s3s.at[half, sem], s3r.at[half, piece, q], (rr, c))

    def post_second(half, piece, m):
        plus = along(axes[half][1], 1)
        minus = along(axes[half][1], 3)
        second(half, piece, 0, plus, 6 * m).start()
        second(half, piece, 1, minus, 6 * m + 1).start()
        second(half, piece, 1, plus, 6 * m + 2).start()
        second(half, piece, 0, minus, 6 * m + 3).start()

    def relay_second(half, d, m):
        for q, side, onward in ((0, 3, 1), (1, 1, 3)):
            if axes[half][0] == "x":
                piece = rem(x + d, 4) * 4 + rem(z + side, 4)
            else:
                piece = rem(x + side, 4) * 4 + rem(z + d, 4)
            second(half, piece, q, r, 0).wait_recv()
            second(half, piece, q, along(axes[half][1], onward), 6 * m + 4 + q).start()

    def settle(half, piece, distance):
        @pl.when(distance != 3)
        def _():
            second(half, piece, 0, r, 0).wait_recv()

        @pl.when(distance != 1)
        def _():
            second(half, piece, 1, r, 0).wait_recv()

    for half in range(2):
        for src_r in range(RSRC):
            @pl.when(r != src_r)
            def _():
                s1(half, r, src_r, 0).wait_recv()

            if half == 0:
                @pl.when(r == src_r)
                def _():
                    own_s().wait()
        for n, d in enumerate(STEPS):
            first(half, r, along(axes[half][0], d), n).start()
        post_second(half, r, 0)

    post_relays(b3)
    for half in range(2):
        relay_second(half, 0, 0)
    for m, d in enumerate(STEPS):
        for half in range(2):
            piece = along(axes[half][0], d)
            first(half, piece, r, 0).wait_recv()
            post_second(half, piece, 1 + m)
    post_relays(t3)
    post_far(b3)
    for half in range(2):
        relay_second(half, STEPS[0], 1)
    post_far(t3)

    def relay_both(m):
        for half in range(2):
            relay_second(half, STEPS[m], 1 + m)

    relay_both(1)
    wait_other(t3)

    core = core_ref[...]
    eliminate(tall, core, state, lmat, rmat, {2: lambda: relay_both(2)})

    wait_other(b3)

    def left_rows(i, carry):
        panel = r * (ROWS // PB) + i
        block = jnp.concatenate([ball[i * 4 + h] for h in range(4)], axis=0)
        for q in range(RSRC):
            lo, hi = q * 2 * SK, (q + 1) * 2 * SK
            out = jnp.dot(block[:, :hi], lmat[:hi, lo:hi], preferred_element_type=f32)
            for j in range(2):
                part = out[:, j * SK : (j + 1) * SK]
                part = jnp.where(2 * q + j < panel, part, jnp.zeros_like(part))
                left[pl.ds(pl.multiple_of(i * PB, PB), PB), lo + j * SK : lo + (j + 1) * SK] = part.astype(bf16)
        return carry

    lax.fori_loop(0, ROWS // PB, left_rows, 0)

    def right_block(i, carry):
        dx = i + div(i, 2) - 2 * div(i, 3)
        xx = rem(x + dx, 4)
        for zz in range(4):
            piece = xx * 4 + zz
            dz = rem(zz - z + 4, 4)

            @pl.when(dz != 0)
            def _():
                settle(0, piece, dz)

            @pl.when(dx != 0)
            def _():
                settle(1, piece, dx)

        block = jnp.concatenate([sall[xx * 4 + h].reshape(RANK, TILE) for h in range(4)], axis=1)
        panel = c * (COLS // PB) + xx
        for q in range(RSRC):
            lo, hi = q * 2 * SK, (q + 1) * 2 * SK
            out = jnp.dot(rmat[lo:hi, :hi], block[:hi], preferred_element_type=f32)
            for j in range(2):
                part = out[j * SK : (j + 1) * SK]
                part = jnp.where(2 * q + j < panel, part, jnp.zeros_like(part))
                right[xx, lo + j * SK : lo + (j + 1) * SK, :] = part.astype(bf16)
        return carry

    lax.fori_loop(0, BLOCKS, right_block, 0)

    @pl.when(r < RSRC)
    def _():
        for src_c in range(CSRC):
            @pl.when(c == src_c)
            def _():
                for i in range(1, NC):
                    t1(rem(c + i, NC), src_c, i).wait_send()
        for i in range(1, NR):
            for half in range(2):
                s1(half, rem(r + i, NR), r, i).wait_send()

    for src_c in range(CSRC):
        @pl.when(c == src_c)
        def _():
            for i in range(1, NC):
                b1(rem(c + i, NC), src_c, i).wait_send()
    for src_r, (hx, hz) in enumerate(homes):
        leg = 0 if src_r < 4 else 3

        @pl.when(r == src_r)
        def _():
            for n in range(3):
                t2(src_r, rem(r + 1, NR), leg + n).wait_send()

        @pl.when((z == hz) if src_r < 4 else (x == hx))
        def _():
            for n in range(3):
                t2(src_r, rem(r + 1, NR), 3 - leg + n).wait_send()
    for i in range(14):
        t3(c, 0, other, i).wait_send()
        b3(c, 0, other, i).wait_send()
    for half in range(2):
        for i in range(3):
            first(half, r, rem(r + 1, NR), i).wait_send()
        for i in range(24):
            second(half, r, 0, rem(r + 1, NR), i).wait_send()


def factors(b, s, t, core):
    vmem = pl.BlockSpec(memory_space=pltpu.VMEM)
    dma = pltpu.SemaphoreType.DMA
    bf16 = jnp.bfloat16
    return pl.pallas_call(
        factor_kernel,
        out_shape=(
            jax.ShapeDtypeStruct((ROWS, RANK), bf16),
            jax.ShapeDtypeStruct((BLOCKS, RANK, WIDE), bf16),
        ),
        in_specs=[vmem] * 4,
        out_specs=(vmem, vmem),
        scratch_shapes=[
            pltpu.VMEM((NC, TILE, RANK), bf16),
            pltpu.VMEM((NR, RSRC, 2 * SK, TILE), bf16),
            pltpu.VMEM((NC, RSRC, TR, RANK), bf16),
            pltpu.VMEM((RANK, RANK), jnp.float32),
            pltpu.VMEM((RANK, RANK), bf16),
            pltpu.VMEM((RANK, RANK), bf16),
            dma((3,)),
            dma((NC,)), dma((CSRC,)), dma((RSRC, 6)), dma((RSRC,)), dma((14,)), dma((NC, 2)),
            dma((NC,)), dma((CSRC,)), dma((14,)), dma((NC, 2)),
            dma((2, NR)), dma((2, RSRC)), dma((2, 3)), dma((2, NR)), dma((2, 24)), dma((2, NR, 2)),
        ],
        compiler_params=pltpu.CompilerParams(
            collective_id=1, has_side_effects=True, vmem_limit_bytes=34 * MIB
        ),
        name="panel_factors",
    )(b, s, t, core)


UR = 512


def update_kernel(left, right, grid, out_ref, obuf, osem):
    f32 = jnp.float32
    n = ROWS // UR

    def of_rows(i):
        return pl.ds(pl.multiple_of(i * UR, UR), UR)

    def store(i, q):
        cols = pl.ds(pl.multiple_of(q * WIDE, WIDE), WIDE)
        return pltpu.make_async_copy(obuf.at[i, :, cols], out_ref.at[of_rows(i), cols], osem.at[i, q])

    def rows(i, carry):
        def block(q, carry):
            cols = pl.ds(pl.multiple_of(q * WIDE, WIDE), WIDE)
            product = jnp.dot(left[of_rows(i), :], right[q], preferred_element_type=f32)
            obuf[i, :, cols] = (grid[of_rows(i), cols] - product).astype(jnp.bfloat16)
            store(i, q).start()
            return carry

        lax.fori_loop(0, BLOCKS, block, 0)
        return carry

    lax.fori_loop(0, n, rows, 0)
    for i in range(n):
        for q in range(BLOCKS):
            store(i, q).wait()


def update(left, right, grid):
    hbm = pl.BlockSpec(memory_space=pltpu.HBM)
    vmem = pl.BlockSpec(memory_space=pltpu.VMEM)
    n = ROWS // UR
    return pl.pallas_call(
        update_kernel,
        out_shape=jax.ShapeDtypeStruct((ROWS, COLS), jnp.bfloat16),
        in_specs=[vmem, vmem, vmem],
        out_specs=hbm,
        scratch_shapes=[pltpu.VMEM((n, UR, COLS), jnp.bfloat16), pltpu.SemaphoreType.DMA((n, BLOCKS))],
        compiler_params=pltpu.CompilerParams(vmem_limit_bytes=12 * MIB),
        name="panel_update",
    )(left, right, grid)


def shards(front, tiles, counts, dest_owner, dest_slot, omega, psi, core):
    owners = dest_owner[:, 0]
    strip = jnp.arange(ND, dtype=jnp.int32)
    same = owners[:, None] == owners[None, :]
    before = strip[None, :] < strip[:, None]
    ranks = jnp.sum((same & before).astype(jnp.int32), axis=1)
    valid = strip < counts[0]
    named = strip[None, :, None] == owners[None, None, :]
    hit = named & (ranks[None, None, :] == jnp.arange(CAP, dtype=jnp.int32)[:, None, None])
    idx = jnp.sum(jnp.where(hit, strip[None, None, :], 0), axis=2)
    slots = jnp.max(jnp.where(hit & valid[None, None, :], dest_slot[None, None, :], -1), axis=2)
    slots = jnp.pad(slots.T[:, None, :], ((0, 0), (0, 0), (0, TILE - CAP)))
    got, got_slots = exchange(idx, slots, tiles)
    grid, b, s, t = assemble(got_slots[:, 0, :], front, got, omega, psi)
    left, right = factors(b, s, t, core)
    return update(left, right, grid)


def solution(mesh):
    in_specs = (
        P("row", "col"),
        P(("row", "col"), None, None),
        P(("row", "col")),
        P(("row", "col"), None),
        P(("row", "col")),
        P(),
        P(),
        P(),
    )
    out_specs = P("row", "col")
    return jax.shard_map(shards, mesh=mesh, in_specs=in_specs, out_specs=out_specs, check_vma=False)
```
